128 devices in a mesh: space: 128 (over x, y, z, core).
Axes of the slice: x: 4, y: 4, z: 4, core: 2. Of those that a mesh axis runs over, the one named last changes fastest.
Arguments:
- state: float32 [131072, 1024], P('space'), may hold values from -6 to 6
- obs_value: float32 [65536], P('space'), may hold values from -6 to 6
- obs_sigma: float32 [65536], P('space'), may hold values from 0.3 to 1.5
- obs_noise: float32 [65536, 1024], P('space'), may hold values from -6 to 6
- obs_pos: int32 [2, 65536], P(None, 'space'), may hold values from 0 to 511, as said below
- obs_side: int32 [65536], P('space'), may hold values from 0 to 1
Outputs:
- predicted_states: float32 [131072, 1024], P('space')
The draws below stay inside these ranges and needn't reach their ends.
Inputs may be any that keep to these rules, and one draw needn't show every extreme that they name: `obs_pos`: observation o lies in grid row (o // 512) * 4 plus 0 to 3; its column is 0 to 255.
All inputs are finite; a program needn't handle non-finite values.
Results may differ from the reference program's by a relative error of at most 0.0038.
Values may be sent and summed in bfloat16 or wider, within the bound.
No kernel may reach another device: no remote copies, remote signals or barrier semaphores. Data moves between devices by JAX's collectives and lax.ppermute only.
A program may use at most 128 MiB of HBM per device.

```python
import math
import jax
import jax.numpy as jnp
from jax import lax

M = 1024
MESH_WIDTH = 256
ROWS_DEV = 4
OBS_DEV = 512
REACH = 4
CELL_DEV = 1024
CELLS = 131072
OBS = 65536
N_SPACE = 128


def draw_obs_pos(key, part):
    first_key, second_key = jax.random.split(jax.random.fold_in(key, 17))
    block_number = jnp.arange(OBS, dtype=jnp.int32) // OBS_DEV
    obs_row = block_number * ROWS_DEV + jax.random.randint(first_key, (OBS,), 0, ROWS_DEV)
    obs_col = jax.random.randint(second_key, (OBS,), 0, MESH_WIDTH)
    return jnp.stack([obs_row, obs_col]).astype(jnp.int32)


def place_ends(entries, rng, least, largest):
    shape = entries.shape
    index_at = [jax.random.randint(jax.random.fold_in(rng, axis), (), 0, shape[axis]) for axis in range(len(shape))]
    entries = entries.at[tuple(index_at)].set(least)
    longest = shape.index(max(shape))
    index_at[longest] = (index_at[longest] + 1) % shape[longest]
    return entries.at[tuple(index_at)].set(largest)


def steps_of(stream_key, dims, cuts, least, top_value):
    factor_of = 1.0
    for position, shards_of in cuts:
        draws = jax.random.uniform(jax.random.fold_in(jax.random.fold_in(stream_key, 6), position), (shards_of,), jnp.float32, least / len(cuts), top_value / len(cuts))
        factor_of = factor_of * jnp.repeat(jnp.exp(draws), dims[position] // shards_of).reshape((-1,) + (1,) * (len(dims) - 1 - position))
    return factor_of


def bell_draw(rng, dims, deviation, most, cuts=(), held_as=jnp.bfloat16):
    entries = jax.random.normal(rng, dims, jnp.float32) * deviation
    if len(cuts) > 0:
        entries = steps_of(rng, dims, cuts, -0.22, 0.18) * entries
    return jnp.clip(entries, min=-most, max=most).astype(held_as)


def setup_inputs(seed: int = 0) -> dict:
    streams_of = jax.random.split(jax.random.key(seed), 7)
    return {
        "state": bell_draw(streams_of[0], (CELLS, M), 1.0, 6.0, ((0, 128),), jnp.float32),
        "obs_value": bell_draw(streams_of[1], (OBS,), 1.0, 6.0, ((0, 128),), jnp.float32),
        "obs_sigma": jnp.clip(jnp.exp(math.log(1.5) - 1.60943787 * jax.random.uniform(streams_of[2], (OBS,), jnp.float32) ** steps_of(streams_of[2], (OBS,), ((0, 128),), -0.2, 0.2)), 0.3, 1.5),
        "obs_noise": bell_draw(streams_of[3], (OBS, M), 1.0, 6.0, ((0, 128),), jnp.float32),
        "obs_pos": draw_obs_pos(jax.random.fold_in(streams_of[6], 71), 0),
        "obs_side": place_ends(jax.random.randint(streams_of[5], (OBS,), 0, 2), jax.random.fold_in(streams_of[5], 1), 0, 1).astype(jnp.int32),
    }


def gaspari(scaled):
    safe = jnp.maximum(scaled, 1.0)
    near_part = -0.25 * scaled ** 5 + 0.5 * scaled ** 4 + 0.625 * scaled ** 3 - 5.0 / 3.0 * scaled ** 2 + 1.0
    far_part = scaled ** 5 / 12.0 - 0.5 * scaled ** 4 + 0.625 * scaled ** 3 + 5.0 / 3.0 * scaled ** 2 - 5.0 * scaled + 4.0 - 2.0 / (3.0 * safe)
    return jnp.where(scaled <= 1.0, near_part, jnp.where(scaled <= 2.0, far_part, 0.0 * scaled))

def contribution(running_sum, state_anom, cell_row, cell_col, obs_anom, weights, obs_pos, mesh_height, sample_states):
    row_gap = jnp.abs(cell_row[:, None] - obs_pos[0][None, :])
    row_gap = jnp.minimum(row_gap, mesh_height - row_gap)
    col_gap = jnp.abs(cell_col[:, None] - obs_pos[1][None, :])
    col_gap = jnp.minimum(col_gap, MESH_WIDTH - col_gap)
    radius = 1.0 * REACH * ROWS_DEV
    scaled = jnp.sqrt((row_gap * row_gap + col_gap * col_gap).astype(jnp.float32)) / radius
    tapers = jnp.where(row_gap <= REACH * ROWS_DEV, gaspari(scaled), 0.0 * scaled)
    covariance = lax.dot_general(state_anom, obs_anom, (((1,), (1,)), ((), ())), preferred_element_type=jnp.float32)
    gain_block = (tapers * covariance / (sample_states - 1)).astype(jnp.bfloat16)
    return running_sum + jnp.dot(gain_block, weights, preferred_element_type=jnp.float32)

def advance_model(state_mesh_entries, row_above, row_below):
    col_right = jnp.roll(state_mesh_entries, -1, axis=1)
    col_left = jnp.roll(state_mesh_entries, 1, axis=1)
    advect_state = 0.05 * state_mesh_entries * (row_above - row_below + (col_right - col_left))
    diffuse_state = 0.2 * (row_above + row_below + col_right + col_left - 4.0 * state_mesh_entries)
    return state_mesh_entries - advect_state + diffuse_state

def reference(state, obs_value, obs_sigma, obs_noise, obs_pos, obs_side):
    sample_states = state.shape[1]
    mesh_height = ROWS_DEV * N_SPACE
    member_mean = lax.optimization_barrier(jnp.mean(state, axis=1, keepdims=True))
    state_anom = (state - member_mean).astype(jnp.bfloat16)
    obs_row = obs_pos[0]
    obs_col = obs_pos[1]
    partner_col = (obs_col + 2 * obs_side - 1) % MESH_WIDTH
    observed = 0.5 * (state[obs_row * MESH_WIDTH + obs_col] + state[obs_row * MESH_WIDTH + partner_col])
    obs_dev = observed - lax.optimization_barrier(jnp.mean(observed, axis=1, keepdims=True))
    obs_anom = obs_dev.astype(jnp.bfloat16)
    spread = lax.optimization_barrier(jnp.sum(obs_dev * obs_dev, axis=1)) / (sample_states - 1)
    innovation = obs_value[:, None] + obs_sigma[:, None] * obs_noise - observed
    weights = (innovation / (spread + obs_sigma * obs_sigma)[:, None]).astype(jnp.bfloat16)
    anom_blocks = obs_anom.reshape(N_SPACE, OBS_DEV, sample_states)
    weight_blocks = weights.reshape(N_SPACE, OBS_DEV, sample_states)
    pos_blocks = obs_pos.reshape(2, N_SPACE, OBS_DEV).transpose(1, 0, 2)
    local_cells = jnp.arange(CELL_DEV, dtype=jnp.int32)

    def block_increment(block_index):
        slab_anom = lax.dynamic_slice_in_dim(state_anom, (block_index * CELL_DEV).astype(jnp.int32), CELL_DEV, 0)
        cell_row = block_index * ROWS_DEV + local_cells // MESH_WIDTH
        cell_col = local_cells % MESH_WIDTH
        running_sum = jnp.zeros((CELL_DEV, sample_states), jnp.float32)
        for offset in range(-REACH, REACH + 1):
            source = ((block_index + offset) % N_SPACE).astype(jnp.int32)
            running_sum = contribution(running_sum, slab_anom, cell_row, cell_col, anom_blocks[source], weight_blocks[source], pos_blocks[source], mesh_height, sample_states)
        return running_sum
    increments = lax.map(block_increment, jnp.arange(N_SPACE, dtype=jnp.int32))
    analysis = state + increments.reshape(mesh_height * MESH_WIDTH, sample_states)
    state_mesh_entries = analysis.reshape(mesh_height, MESH_WIDTH, sample_states)
    predicted_states = advance_model(state_mesh_entries, jnp.roll(state_mesh_entries, -1, axis=0), jnp.roll(state_mesh_entries, 1, axis=0))
    return predicted_states.reshape(mesh_height * MESH_WIDTH, sample_states)
```

```python
import functools

import jax
import jax.numpy as jnp
from jax import lax
from jax.experimental import pallas as pl
from jax.experimental.pallas import tpu as pltpu
from jax.sharding import PartitionSpec as P

WIDTH = 256
ROWS = 4
REACH = 4
CELLS = ROWS * WIDTH
OBS = 512
M = 1024
CHUNK = 16
VMEM = 48 * 1024 * 1024
F32 = jnp.float32
BF16 = jnp.bfloat16


def params():
    return pltpu.CompilerParams(vmem_limit_bytes=VMEM, dimension_semantics=("arbitrary",))


def cost(flops, nbytes):
    return pl.CostEstimate(flops=int(flops), bytes_accessed=int(nbytes), transcendentals=0)


def column(row):
    return jnp.broadcast_to(row, (8, row.shape[1])).T[:, 0:1]


def prep_kernel(row0_ref, state_ref, pos_ref, side_ref, x_ref, a_ref, dev_ref, mean_ref, hi_scr, lo_scr, m_scr):
    r = pl.program_id(0)
    s = state_ref[...]
    ms = jnp.mean(s, axis=1, keepdims=True)
    sd = s - ms
    x_ref[...] = sd.astype(BF16)
    dev = 0.5 * (sd + pltpu.roll(sd, WIDTH - 1, 0))
    hi = dev.astype(BF16)
    here = pl.ds(pl.multiple_of(r * WIDTH, WIDTH), WIDTH)
    hi_scr[here, :] = hi
    lo_scr[here, :] = (dev - hi.astype(F32)).astype(BF16)
    mw = jnp.broadcast_to(ms, (WIDTH, 128))
    pm = 0.5 * (mw + pltpu.roll(mw, WIDTH - 1, 0))
    p0 = pm.astype(BF16).astype(F32)
    p1 = (pm - p0).astype(BF16).astype(F32)
    p2 = pm - p0 - p1
    lane = lax.broadcasted_iota(jnp.int32, (WIDTH, 128), 1)
    m_scr[here, :] = jnp.where(
        lane == 0, p0, jnp.where(lane == 1, p1, jnp.where(lane == 2, p2, 0.0))
    ).astype(BF16)

    @pl.when(r == ROWS - 1)
    def _():
        local = pos_ref[0:1, :] - row0_ref[0]
        col = pos_ref[1:2, :]
        left = (col + side_ref[...] - 1) & (WIDTH - 1)
        index = column((local * WIDTH + left).astype(F32)).astype(jnp.int32)
        cells = lax.broadcasted_iota(jnp.int32, (OBS, CELLS), 1)
        pick = jnp.where(cells == index, 1.0, 0.0).astype(BF16)
        for n in range(4):
            part = slice(n * 256, (n + 1) * 256)
            high = jnp.dot(pick, hi_scr[:, part], preferred_element_type=F32)
            low = jnp.dot(pick, lo_scr[:, part], preferred_element_type=F32)
            a_ref[0:OBS, part] = high.astype(BF16)
            dev_ref[:, part] = high + low
        mg = jnp.dot(pick, m_scr[...], preferred_element_type=F32)
        mean_ref[...] = jnp.broadcast_to(jnp.sum(mg, axis=1, keepdims=True), (OBS, 128))
        sub = lax.broadcasted_iota(jnp.int32, (16, OBS), 0)
        code = jnp.where(sub == 0, local.astype(F32), jnp.where(sub == 1, col.astype(F32), 0.0))
        a_ref[OBS : OBS + 16, 0:OBS] = code.astype(BF16)
        a_ref[OBS : OBS + 16, OBS:M] = jnp.zeros((16, M - OBS), BF16)


def prep(row0, state, pos, side):
    full = lambda shape: pl.BlockSpec(shape, lambda r: (0,) * len(shape))
    return pl.pallas_call(
        prep_kernel,
        grid=(ROWS,),
        in_specs=[
            pl.BlockSpec(memory_space=pltpu.SMEM),
            pl.BlockSpec((WIDTH, M), lambda r: (r, 0)),
            full((2, OBS)),
            full((1, OBS)),
        ],
        out_specs=[
            pl.BlockSpec((WIDTH, M), lambda r: (r, 0)),
            full((OBS + 16, M)),
            full((OBS, M)),
            full((OBS, 128)),
        ],
        out_shape=[
            jax.ShapeDtypeStruct((CELLS, M), BF16),
            jax.ShapeDtypeStruct((OBS + 16, M), BF16),
            jax.ShapeDtypeStruct((OBS, M), F32),
            jax.ShapeDtypeStruct((OBS, 128), F32),
        ],
        scratch_shapes=[
            pltpu.VMEM((CELLS, M), BF16),
            pltpu.VMEM((CELLS, M), BF16),
            pltpu.VMEM((CELLS, 128), BF16),
        ],
        compiler_params=params(),
        cost_estimate=cost(4 * OBS * CELLS * M, 10 << 20),
        name="prep",
    )(row0, state, pos, side)


def weight_kernel(dev_ref, mean_ref, value_ref, sigma_ref, noise_ref, w_ref):
    dev = dev_ref[...]
    spread = jnp.sum(dev * dev, axis=1, keepdims=True) * (1.0 / (M - 1))
    value = column(value_ref[...])
    sigma = column(sigma_ref[...])
    scale = 1.0 / (spread + sigma * sigma)
    base = value - mean_ref[:, 0:1]
    w_ref[...] = ((base + sigma * noise_ref[...] - dev) * scale).astype(BF16)


def weigh(dev, mean, value, sigma, noise):
    rows = 128
    return pl.pallas_call(
        weight_kernel,
        grid=(OBS // rows,),
        in_specs=[
            pl.BlockSpec((rows, M), lambda i: (i, 0)),
            pl.BlockSpec((rows, 128), lambda i: (i, 0)),
            pl.BlockSpec((1, rows), lambda i: (0, i)),
            pl.BlockSpec((1, rows), lambda i: (0, i)),
            pl.BlockSpec((rows, M), lambda i: (i, 0)),
        ],
        out_specs=pl.BlockSpec((rows, M), lambda i: (i, 0)),
        out_shape=jax.ShapeDtypeStruct((OBS, M), BF16),
        compiler_params=params(),
        cost_estimate=cost(8 * OBS * M, 5 << 20),
        name="weigh",
    )(dev, mean, value, sigma, noise)


def gain_rows(r, x, a_ref, offset, cov_scr, put):
    cov_scr[...] = lax.dot_general(
        x, a_ref[0:OBS, :], (((1,), (1,)), ((), ())), preferred_element_type=F32
    )
    code = a_ref[OBS : OBS + 16, 0:OBS].astype(F32)
    gap = jnp.abs(code[0:1, :] + (ROWS * offset - r).astype(F32))
    row2 = jnp.where(gap > REACH * ROWS, 1e4, gap * gap * (1.0 / 256.0))
    col = code[1:2, :] * (1.0 / 16.0)
    n1 = 1.0 / (M - 1)
    for i in range(WIDTH // CHUNK):
        rows = slice(i * CHUNK, (i + 1) * CHUNK)
        q = (lax.broadcasted_iota(jnp.int32, (CHUNK, 1), 0) + i * CHUNK).astype(F32) * (1.0 / 16.0)
        d = jnp.abs(q - col)
        d = jnp.minimum(d, 16.0 - d)
        z2 = d * d + row2
        inv = lax.rsqrt(jnp.maximum(z2, 1e-9))
        z = z2 * inv
        near = z2 * (z * ((0.625 * n1) + z * ((0.5 * n1) - (0.25 * n1) * z)) - (5.0 / 3.0 * n1)) + n1
        u = jnp.maximum(2.0 - z, 0.0)
        u2 = u * u
        far = (u2 * u2) * (z2 + (2.0 * z - 0.5)) * (inv * (n1 / 12.0))
        put(rows, (jnp.where(z2 <= 1.0, near, far) * cov_scr[rows, :]).astype(BF16))


def contribute_kernel(offsets, first, *refs):
    n = len(offsets)
    x_ref = refs[0]
    a_refs = refs[1 : 1 + n]
    w_refs = refs[1 + n : 1 + 2 * n]
    acc_ref = refs[1 + 2 * n]
    out_ref, cov_scr, g_scr = refs[-3:]
    r = pl.program_id(0)
    x = x_ref[...]
    total = acc_ref[...]
    for k, offset in enumerate(offsets):

        def put(rows, val):
            g_scr[rows, :] = val

        gain_rows(r, x, a_refs[k], offset, cov_scr, put)
        total = total + jnp.dot(g_scr[...], w_refs[k][...], preferred_element_type=F32)
    out_ref[...] = total


def contribute(x, packets, weights, offsets, acc, first):
    n = len(offsets)
    tile = pl.BlockSpec((WIDTH, M), lambda r: (r, 0))
    whole = lambda rows: pl.BlockSpec((rows, M), lambda r: (0, 0))
    return pl.pallas_call(
        functools.partial(contribute_kernel, offsets, first),
        grid=(ROWS,),
        in_specs=[tile] + [whole(OBS + 16)] * n + [whole(OBS)] * n + [tile],
        out_specs=tile,
        out_shape=jax.ShapeDtypeStruct((CELLS, M), F32),
        scratch_shapes=[pltpu.VMEM((WIDTH, OBS), F32), pltpu.VMEM((WIDTH, OBS), BF16)],
        input_output_aliases={} if first else {1 + 2 * n: 0},
        compiler_params=params(),
        cost_estimate=cost(8 * n * CELLS * OBS * M, 10 << 20),
        name="contribute",
    )(x, *packets, *weights, acc)


def gain_kernel(offsets, x_ref, au_ref, ad_ref, g_ref, cov_scr):
    r = pl.program_id(0)
    x = x_ref[...]
    for k, (a_ref, offset) in enumerate(zip((au_ref, ad_ref), offsets)):

        def put(rows, val, k=k):
            g_ref[rows, k * OBS : (k + 1) * OBS] = val

        gain_rows(r, x, a_ref, offset, cov_scr, put)


def gains(x, packets, offsets):
    tile = pl.BlockSpec((WIDTH, M), lambda r: (r, 0))
    whole = pl.BlockSpec((OBS + 16, M), lambda r: (0, 0))
    return pl.pallas_call(
        functools.partial(gain_kernel, offsets),
        grid=(ROWS,),
        in_specs=[tile, whole, whole],
        out_specs=pl.BlockSpec((WIDTH, 2 * OBS), lambda r: (r, 0)),
        out_shape=jax.ShapeDtypeStruct((CELLS, 2 * OBS), BF16),
        scratch_shapes=[pltpu.VMEM((WIDTH, OBS), F32)],
        compiler_params=params(),
        cost_estimate=cost(8 * CELLS * OBS * M, 6 << 20),
        name="gains",
    )(x, *packets)


def edge_kernel(acc_ref, g_ref, wu_ref, wd_ref, out_ref, send_ref):
    total = acc_ref[...]
    total = total + jnp.dot(g_ref[:, 0:OBS], wu_ref[...], preferred_element_type=F32)
    total = total + jnp.dot(g_ref[:, OBS : 2 * OBS], wd_ref[...], preferred_element_type=F32)
    out_ref[...] = total
    send_ref[0] = total.astype(BF16)


def edges(acc, gain, wu, wd):
    tile = pl.BlockSpec((WIDTH, M), lambda i: (3 * i, 0))
    whole = pl.BlockSpec((OBS, M), lambda i: (0, 0))
    return pl.pallas_call(
        edge_kernel,
        grid=(2,),
        in_specs=[tile, tile, whole, whole],
        out_specs=[
            pl.BlockSpec((WIDTH, M), lambda i: (i, 0)),
            pl.BlockSpec((1, WIDTH, M), lambda i: (i, 0, 0)),
        ],
        out_shape=[
            jax.ShapeDtypeStruct((2 * WIDTH, M), F32),
            jax.ShapeDtypeStruct((2, WIDTH, M), BF16),
        ],
        compiler_params=params(),
        cost_estimate=cost(4 * CELLS * OBS * M, 6 << 20),
        name="edges",
    )(acc, gain, wu, wd)


def advance(a, above, below):
    right = pltpu.roll(a, WIDTH - 1, 0)
    left = pltpu.roll(a, 1, 0)
    pull = 0.05 * a * (above - below + (right - left))
    spread = 0.2 * (above + below + right + left - 4.0 * a)
    return a - pull + spread


def inner_kernel(acc_ref, g_ref, wu_ref, wd_ref, edge_ref, mid_ref, out_ref):
    i = pl.program_id(0)
    lanes = pl.ds(pl.multiple_of(i * 256, 256), 256)
    total = acc_ref[WIDTH : 3 * WIDTH, :]
    total = total + jnp.dot(
        g_ref[WIDTH : 3 * WIDTH, 0:OBS], wu_ref[...], preferred_element_type=F32
    )
    total = total + jnp.dot(
        g_ref[WIDTH : 3 * WIDTH, OBS : 2 * OBS], wd_ref[...], preferred_element_type=F32
    )
    mid_ref[...] = total
    one = total[0:WIDTH]
    two = total[WIDTH : 2 * WIDTH]
    out_ref[0:WIDTH, :] = advance(one, two, edge_ref[0:WIDTH, :])
    out_ref[WIDTH : 2 * WIDTH, :] = advance(two, edge_ref[WIDTH : 2 * WIDTH, :], one)


def inner(acc, gain, wu, wd, edge):
    cols = lambda rows: pl.BlockSpec((rows, 256), lambda i: (0, i))
    return pl.pallas_call(
        inner_kernel,
        grid=(M // 256,),
        in_specs=[
            cols(CELLS),
            pl.BlockSpec((CELLS, 2 * OBS), lambda i: (0, 0)),
            cols(OBS),
            cols(OBS),
            cols(2 * WIDTH),
        ],
        out_specs=[cols(2 * WIDTH), cols(2 * WIDTH)],
        out_shape=[
            jax.ShapeDtypeStruct((2 * WIDTH, M), F32),
            jax.ShapeDtypeStruct((2 * WIDTH, M), F32),
        ],
        compiler_params=params(),
        cost_estimate=cost(4 * CELLS * OBS * M, 10 << 20),
        name="inner",
    )(acc, gain, wu, wd, edge)


def outer_kernel(edge_ref, mid_ref, before_ref, after_ref, pred_ref, out_ref):
    first = edge_ref[0:WIDTH, :]
    last = edge_ref[WIDTH : 2 * WIDTH, :]
    one = mid_ref[0:WIDTH, :]
    two = mid_ref[WIDTH : 2 * WIDTH, :]
    out_ref[0:WIDTH, :] = advance(first, one, before_ref[0].astype(F32))
    out_ref[WIDTH : 3 * WIDTH, :] = pred_ref[...]
    out_ref[3 * WIDTH : 4 * WIDTH, :] = advance(last, after_ref[0].astype(F32), two)


def outer(edge, mid, before, after, pred):
    cols = lambda rows: pl.BlockSpec((rows, 256), lambda i: (0, i))
    halo = pl.BlockSpec((1, WIDTH, 256), lambda i: (0, 0, i))
    return pl.pallas_call(
        outer_kernel,
        grid=(M // 256,),
        in_specs=[cols(2 * WIDTH), cols(2 * WIDTH), halo, halo, cols(2 * WIDTH)],
        out_specs=cols(CELLS),
        out_shape=jax.ShapeDtypeStruct((CELLS, M), F32),
        compiler_params=params(),
        cost_estimate=cost(20 * CELLS * M, 12 << 20),
        name="outer",
    )(edge, mid, before, after, pred)


def on_device(state, obs_value, obs_sigma, obs_noise, obs_pos, obs_side):
    device = lax.axis_index("space")
    slabs = lax.axis_size("space")
    up = [(i, (i + 1) % slabs) for i in range(slabs)]
    down = [(j, i) for i, j in up]
    row0 = (device * ROWS).astype(jnp.int32).reshape(1)
    x, a, dev, mean = prep(row0, state, obs_pos, obs_side.reshape(1, OBS))
    w = weigh(dev, mean, obs_value.reshape(1, OBS), obs_sigma.reshape(1, OBS), obs_noise)
    acc = contribute(x, (a,), (w,), (0,), state, True)
    lower_a = upper_a = a
    lower_w = upper_w = w
    for step in range(1, REACH + 1):
        lower_a = lax.ppermute(lower_a, "space", up)
        upper_a = lax.ppermute(upper_a, "space", down)
        lower_w = lax.ppermute(lower_w, "space", up)
        upper_w = lax.ppermute(upper_w, "space", down)
        if step < REACH:
            acc = contribute(
                x, (lower_a, upper_a), (lower_w, upper_w), (-step, step), acc, False
            )
    gain = gains(x, (lower_a, upper_a), (-REACH, REACH))
    edge, send = edges(acc, gain, lower_w, upper_w)
    before = lax.ppermute(send[1:2], "space", up)
    after = lax.ppermute(send[0:1], "space", down)
    mid, pred = inner(acc, gain, lower_w, upper_w, edge)
    return outer(edge, mid, before, after, pred)


def solution(mesh):
    placed = (
        P("space", None),
        P("space"),
        P("space"),
        P("space", None),
        P(None, "space"),
        P("space"),
    )
    return jax.shard_map(
        on_device, mesh=mesh, in_specs=placed, out_specs=P("space", None), check_vma=False
    )
```

```python
import functools

import jax
import jax.numpy as jnp
from jax import lax
from jax.experimental import pallas as pl
from jax.experimental.pallas import tpu as pltpu
from jax.sharding import PartitionSpec as P

WIDTH = 256
ROWS = 4
REACH = 4
CELLS = ROWS * WIDTH
OBS = 512
M = 1024
CHUNK = 16
PREP_VMEM = 61 * 1024 * 1024
VMEM = 20 * 1024 * 1024
F32 = jnp.float32
BF16 = jnp.bfloat16


def params():
    return pltpu.CompilerParams(vmem_limit_bytes=VMEM)


def cost(flops, nbytes):
    return pl.CostEstimate(flops=int(flops), bytes_accessed=int(nbytes), transcendentals=0)


def column(row):
    return jnp.broadcast_to(row, (8, row.shape[1])).T[:, 0:1]


def prep_kernel(
    row0_ref, state_ref, pos_ref, side_ref, value_ref, sigma_ref, noise_ref,
    x_ref, p_ref, w_ref, hi_scr, lo_scr, m_scr, noise_scr, sem,
):
    r = pl.program_id(0)
    fetch = pltpu.make_async_copy(noise_ref, noise_scr, sem)

    @pl.when(r == 0)
    def _():
        fetch.start()

    s = state_ref[...]
    ms = jnp.mean(s, axis=1, keepdims=True)
    sd = s - ms
    x_ref[...] = sd.astype(BF16)
    dev = 0.5 * (sd + pltpu.roll(sd, WIDTH - 1, 0))
    hi = dev.astype(BF16)
    here = pl.ds(pl.multiple_of(r * WIDTH, WIDTH), WIDTH)
    hi_scr[here, :] = hi
    lo_scr[here, :] = (dev - hi.astype(F32)).astype(BF16)
    mw = jnp.broadcast_to(ms, (WIDTH, 128))
    pm = 0.5 * (mw + pltpu.roll(mw, WIDTH - 1, 0))
    p0 = pm.astype(BF16).astype(F32)
    p1 = (pm - p0).astype(BF16).astype(F32)
    p2 = pm - p0 - p1
    lane = lax.broadcasted_iota(jnp.int32, (WIDTH, 128), 1)
    m_scr[here, :] = jnp.where(
        lane == 0, p0, jnp.where(lane == 1, p1, jnp.where(lane == 2, p2, 0.0))
    ).astype(BF16)

    @pl.when(r == ROWS - 1)
    def _():
        local = pos_ref[0:1, :] - row0_ref[0]
        col = pos_ref[1:2, :]
        left = (col + side_ref[...] - 1) & (WIDTH - 1)
        sub = lax.broadcasted_iota(jnp.int32, (16, OBS), 0)
        code = jnp.where(sub == 0, local.astype(F32), jnp.where(sub == 1, col.astype(F32), 0.0))
        p_ref[OBS : OBS + 16, 0:OBS] = code.astype(BF16)
        p_ref[OBS : OBS + 16, OBS:M] = jnp.zeros((16, M - OBS), BF16)
        index = column((local * WIDTH + left).astype(F32)).astype(jnp.int32)
        value = column(value_ref[...])
        sigma = column(sigma_ref[...])
        fetch.wait()
        for b in range(4):
            obs = slice(b * 128, (b + 1) * 128)
            cells = lax.broadcasted_iota(jnp.int32, (128, CELLS), 1)
            pick = jnp.where(cells == index[obs], 1.0, 0.0).astype(BF16)
            high = jnp.dot(pick, hi_scr[...], preferred_element_type=F32)
            low = jnp.dot(pick, lo_scr[...], preferred_element_type=F32)
            p_ref[obs, :] = high.astype(BF16)
            dev_o = high + low
            mg = jnp.dot(pick, m_scr[...], preferred_element_type=F32)
            base = value[obs] - jnp.sum(mg, axis=1, keepdims=True)
            spread = jnp.sum(dev_o * dev_o, axis=1, keepdims=True) * (1.0 / (M - 1))
            scale = 1.0 / (spread + sigma[obs] * sigma[obs])
            w = (base + sigma[obs] * noise_scr[obs, :] - dev_o) * scale
            w_ref[obs, :] = w.astype(BF16)


def prep(row0, state, pos, side, value, sigma, noise):
    full = lambda shape: pl.BlockSpec(shape, lambda r: (0,) * len(shape))
    tile = pl.BlockSpec((WIDTH, M), lambda r: (r, 0))
    return pl.pallas_call(
        prep_kernel,
        grid=(ROWS,),
        in_specs=[
            pl.BlockSpec(memory_space=pltpu.SMEM),
            tile,
            full((2, OBS)),
            full((1, OBS)),
            full((1, OBS)),
            full((1, OBS)),
            pl.BlockSpec(memory_space=pl.ANY),
        ],
        out_specs=[tile, full((OBS + 16, M)), full((OBS, M))],
        out_shape=[
            jax.ShapeDtypeStruct((CELLS, M), BF16),
            jax.ShapeDtypeStruct((OBS + 16, M), BF16),
            jax.ShapeDtypeStruct((OBS, M), BF16),
        ],
        scratch_shapes=[
            pltpu.VMEM((CELLS, M), BF16),
            pltpu.VMEM((CELLS, M), BF16),
            pltpu.VMEM((CELLS, 128), BF16),
            pltpu.VMEM((OBS, M), F32),
            pltpu.SemaphoreType.DMA,
        ],
        compiler_params=pltpu.CompilerParams(
            vmem_limit_bytes=PREP_VMEM, dimension_semantics=("arbitrary",)
        ),
        cost_estimate=cost(1 << 20, 1 << 16),
        name="prep",
    )(row0, state, pos, side, value, sigma, noise)


def covariance(x, a_ref, cov_ref):
    cov_ref[...] = lax.dot_general(
        x, a_ref[0:OBS, :], (((1,), (1,)), ((), ())), preferred_element_type=F32
    )


def gain_rows(r, a_ref, offset, cov_ref, g_ref):
    code = a_ref[OBS : OBS + 16, 0:OBS].astype(F32)
    gap = jnp.abs(code[0:1, :] + (ROWS * offset - r).astype(F32))
    row2 = jnp.where(gap > REACH * ROWS, 1e4, jnp.maximum(gap * gap * (1.0 / 256.0), 1e-12))
    col = code[1:2, :] * (1.0 / 16.0)
    n1 = 1.0 / (M - 1)
    for i in range(WIDTH // CHUNK):
        rows = slice(i * CHUNK, (i + 1) * CHUNK)
        q = (lax.broadcasted_iota(jnp.int32, (CHUNK, 1), 0) + i * CHUNK).astype(F32) * (1.0 / 16.0)
        d = jnp.abs(q - col)
        d = jnp.minimum(d, 16.0 - d)
        z2 = d * d + row2
        inv = lax.rsqrt(z2)
        z = z2 * inv
        near = z2 * (z * ((0.625 * n1) + z * ((0.5 * n1) - (0.25 * n1) * z)) - (5.0 / 3.0 * n1)) + n1
        u = jnp.maximum(2.0 - z, 0.0)
        u2 = u * u
        far = (u2 * u2) * ((z2 + (2.0 * z - 0.5)) * (inv * (n1 / 12.0)))
        g_ref[rows, :] = (jnp.where(z2 <= 1.0, near, far) * cov_ref[rows, :]).astype(BF16)


def in_vmem():
    return pl.BlockSpec(memory_space=pltpu.VMEM)


def in_smem():
    return pl.BlockSpec(memory_space=pltpu.SMEM)


def contribute_kernel(distances, sign_ref, x_ref, *refs):
    n = len(distances)
    a_refs = refs[0:n]
    w_refs = refs[n : 2 * n]
    acc_ref, out_ref, cov_scr, g_scr = refs[2 * n :]

    @pl.loop(0, ROWS)
    def _(r):
        here = pl.ds(pl.multiple_of(r * WIDTH, WIDTH), WIDTH)
        for k in range(n):
            covariance(x_ref[here, :], a_refs[k], cov_scr.at[k])
        for k, distance in enumerate(distances):
            gain_rows(r, a_refs[k], sign_ref[0] * distance, cov_scr.at[k], g_scr.at[k])
        for h in range(2):
            part = slice(h * (M // 2), (h + 1) * (M // 2))
            total = acc_ref[here, part]
            for k in range(n):
                total = total + jnp.dot(
                    g_scr[k], w_refs[k][:, part], preferred_element_type=F32
                )
            out_ref[here, part] = total


def contribute(sign, x, packets, distances, acc, first=False):
    n = len(distances)
    return pl.pallas_call(
        functools.partial(contribute_kernel, distances),
        in_specs=[in_smem()] + [in_vmem()] * (2 * n + 2),
        out_specs=in_vmem(),
        out_shape=jax.ShapeDtypeStruct((CELLS, M), F32),
        scratch_shapes=[pltpu.VMEM((n, WIDTH, OBS), F32), pltpu.VMEM((n, WIDTH, OBS), BF16)],
        input_output_aliases={} if first else {2 + 2 * n: 0},
        compiler_params=params(),
        cost_estimate=cost(1 << 20, 1 << 16),
        name="contribute",
    )(sign, x, *[a for a, _ in packets], *[w for _, w in packets], acc)


def gain_kernel(distance, sign_ref, x_ref, a_ref, g_ref, cov_scr):
    @pl.loop(0, ROWS)
    def _(r):
        here = pl.ds(pl.multiple_of(r * WIDTH, WIDTH), WIDTH)
        covariance(x_ref[here, :], a_ref, cov_scr)
        gain_rows(r, a_ref, sign_ref[0] * distance, cov_scr, g_ref.at[here])


def gains(sign, x, a, distance):
    return pl.pallas_call(
        functools.partial(gain_kernel, distance),
        in_specs=[in_smem(), in_vmem(), in_vmem()],
        out_specs=in_vmem(),
        out_shape=jax.ShapeDtypeStruct((CELLS, OBS), BF16),
        scratch_shapes=[pltpu.VMEM((WIDTH, OBS), F32)],
        compiler_params=params(),
        cost_estimate=cost(1 << 20, 1 << 16),
        name="gains",
    )(sign, x, a)


def edge_kernel(sign_ref, acc_ref, g_ref, w_ref, out_ref, cross_ref, inner_ref):
    for i in range(2):
        here = slice(3 * i * WIDTH, (3 * i + 1) * WIDTH)
        for h in range(4):
            part = slice(h * (M // 4), (h + 1) * (M // 4))
            total = acc_ref[here, part] + jnp.dot(
                g_ref[here, :], w_ref[:, part], preferred_element_type=F32
            )
            out_ref[here, part] = total
            outward = 2 * i - 1 == sign_ref[0]

            @pl.when(jnp.logical_not(outward))
            def _():
                inner_ref[:, part] = total.astype(BF16)

            @pl.when(outward)
            def _():
                cross_ref[:, part] = total.astype(BF16)


def edges(sign, acc, gain, w):
    return pl.pallas_call(
        edge_kernel,
        in_specs=[in_smem(), in_vmem(), in_vmem(), in_vmem()],
        out_specs=[in_vmem()] * 3,
        out_shape=[
            jax.ShapeDtypeStruct((CELLS, M), F32),
            jax.ShapeDtypeStruct((WIDTH, M), BF16),
            jax.ShapeDtypeStruct((WIDTH, M), BF16),
        ],
        input_output_aliases={1: 0},
        compiler_params=params(),
        cost_estimate=cost(1 << 20, 1 << 16),
        name="edges",
    )(sign, acc, gain, w)


def advance(a, above, below):
    right = pltpu.roll(a, WIDTH - 1, 0)
    left = pltpu.roll(a, 1, 0)
    pull = 0.05 * a * (above - below + (right - left))
    spread = 0.2 * (above + below + right + left - 4.0 * a)
    return a - pull + spread


def middle_kernel(acc_ref, g_ref, w_ref, mid_ref, out_ref, pred_scr, sems):
    rows = lambda r: slice(r * WIDTH, (r + 1) * WIDTH)
    copies = []
    for h in range(4):
        part = slice(h * (M // 4), (h + 1) * (M // 4))
        mids = []
        for i in range(2):
            total = acc_ref[rows(1 + i), part] + jnp.dot(
                g_ref[rows(1 + i), :], w_ref[:, part], preferred_element_type=F32
            )
            mid_ref[rows(i), part] = total
            mids.append(total)
        pred_scr[rows(0), part] = advance(mids[0], mids[1], acc_ref[rows(0), part])
        pred_scr[rows(1), part] = advance(mids[1], acc_ref[rows(3), part], mids[0])
        copies.append(
            pltpu.make_async_copy(
                pred_scr.at[:, part], out_ref.at[WIDTH : 3 * WIDTH, part], sems.at[h]
            )
        )
        copies[-1].start()
    for copy in copies:
        copy.wait()


def middle(acc, gain, w):
    return pl.pallas_call(
        middle_kernel,
        in_specs=[in_vmem()] * 3,
        out_specs=[in_vmem(), pl.BlockSpec(memory_space=pl.ANY)],
        out_shape=[
            jax.ShapeDtypeStruct((2 * WIDTH, M), F32),
            jax.ShapeDtypeStruct((CELLS, M), F32),
        ],
        scratch_shapes=[pltpu.VMEM((2 * WIDTH, M), F32), pltpu.SemaphoreType.DMA((4,))],
        compiler_params=params(),
        cost_estimate=cost(1 << 20, 1 << 16),
        name="middle",
    )(acc, gain, w)


def outer_kernel(sign_ref, acc_ref, mid_ref, cross_ref, inner_ref, _, out_ref, pred_scr, sems):
    rows = lambda r: slice(r * WIDTH, (r + 1) * WIDTH)
    first = sign_ref[0] < 0
    copies = []
    for h in range(4):
        part = slice(h * (M // 4), (h + 1) * (M // 4))
        cross = cross_ref[:, part].astype(F32)
        inner = inner_ref[:, part].astype(F32)
        before = jnp.where(first, cross, inner)
        after = jnp.where(first, inner, cross)
        pred_scr[rows(0), part] = advance(acc_ref[rows(0), part], mid_ref[rows(0), part], before)
        pred_scr[rows(1), part] = advance(acc_ref[rows(3), part], after, mid_ref[rows(1), part])
        for i in range(2):
            copies.append(
                pltpu.make_async_copy(
                    pred_scr.at[rows(i), part], out_ref.at[rows(3 * i), part], sems.at[2 * h + i]
                )
            )
            copies[-1].start()
    for copy in copies:
        copy.wait()


def outer(sign, acc, mid, cross, inner, out):
    return pl.pallas_call(
        outer_kernel,
        in_specs=[in_smem()] + [in_vmem()] * 4 + [pl.BlockSpec(memory_space=pl.ANY)],
        out_specs=pl.BlockSpec(memory_space=pl.ANY),
        out_shape=jax.ShapeDtypeStruct((CELLS, M), F32),
        scratch_shapes=[pltpu.VMEM((2 * WIDTH, M), F32), pltpu.SemaphoreType.DMA((8,))],
        input_output_aliases={5: 0},
        compiler_params=params(),
        cost_estimate=cost(1 << 20, 1 << 16),
        name="outer",
    )(sign, acc, mid, cross, inner, out)


def hold(value, acc):
    held, acc = lax.optimization_barrier((value, acc))
    return held, acc


def on_device(state, obs_value, obs_sigma, obs_noise, obs_pos, obs_side):
    device = lax.axis_index("space")
    slabs = lax.axis_size("space")
    pairs = [(i, i ^ 1) for i in range(slabs)]
    across = [(i, (i + 1 if i % 2 else i - 1) % slabs) for i in range(slabs)]
    inside = lambda block: lax.ppermute(block, "space", pairs)
    beyond = lambda block: lax.ppermute(block, "space", across)
    row0 = (device * ROWS).astype(jnp.int32).reshape(1)
    sign = (2 * (device % 2) - 1).astype(jnp.int32).reshape(1)
    row = lambda v: v.reshape(1, OBS)
    x, own_a, own_w = prep(
        row0, state, obs_pos, row(obs_side), row(obs_value), row(obs_sigma), obs_noise
    )

    one_a, one_w = beyond(own_a), beyond(own_w)
    twin_a, twin_w = inside(own_a), inside(own_w)
    two_a, two_w = beyond(twin_a), beyond(twin_w)
    acc = contribute(sign, x, ((own_a, own_w), (twin_a, twin_w)), (0, -1), state, True)
    one_a, acc = hold(one_a, acc)
    one_twin_a, one_twin_w = inside(one_a), inside(one_w)
    three_a, three_w = beyond(one_twin_a), beyond(one_twin_w)
    acc = contribute(sign, x, ((one_a, one_w), (one_twin_a, one_twin_w)), (1, -2), acc)
    two_a, acc = hold(two_a, acc)
    two_twin_a, two_twin_w = inside(two_a), inside(two_w)
    four_a, four_w = beyond(two_twin_a), beyond(two_twin_w)
    acc = contribute(sign, x, ((two_a, two_w), (two_twin_a, two_twin_w)), (2, -3), acc)
    three_a, acc = hold(three_a, acc)
    three_twin_a, three_twin_w = inside(three_a), inside(three_w)
    acc = contribute(sign, x, ((three_a, three_w), (three_twin_a, three_twin_w)), (3, -4), acc)
    four_a, acc = hold(four_a, acc)
    gain = gains(sign, x, four_a, 4)
    acc, to_cross, to_inner = edges(sign, acc, gain, four_w)
    cross, inner = beyond(to_cross), inside(to_inner)
    mid, out = middle(acc, gain, four_w)
    return outer(sign, acc, mid, cross, inner, out)


def solution(mesh):
    placed = (
        P("space", None),
        P("space"),
        P("space"),
        P("space", None),
        P(None, "space"),
        P("space"),
    )
    return jax.shard_map(
        on_device, mesh=mesh, in_specs=placed, out_specs=P("space", None), check_vma=False
    )
```

```python
import functools

import jax
import jax.numpy as jnp
from jax import lax
from jax.experimental import pallas as pl
from jax.experimental.pallas import tpu as pltpu
from jax.sharding import PartitionSpec as P

WIDTH = 256
ROWS = 4
REACH = 4
CELLS = ROWS * WIDTH
OBS = 512
M = 1024
CHUNK = 16
PREP_VMEM = 61 * 1024 * 1024
VMEM = 20 * 1024 * 1024
F32 = jnp.float32
BF16 = jnp.bfloat16


def params():
    return pltpu.CompilerParams(vmem_limit_bytes=VMEM)


def cost(flops, nbytes):
    return pl.CostEstimate(flops=int(flops), bytes_accessed=int(nbytes), transcendentals=0)


def column(row):
    return jnp.broadcast_to(row, (8, row.shape[1])).T[:, 0:1]


def halves(v):
    high = v.astype(BF16).astype(F32)
    return high, v - high


def anomaly_kernel(
    row0_ref, state_ref, pos_ref, side_ref, value_ref, sigma_ref, x_ref, a_ref, hi_scr, m_scr
):
    r = pl.program_id(0)
    s = state_ref[...]
    ms = jnp.mean(s, axis=1, keepdims=True)
    sd = s - ms
    x_ref[...] = sd.astype(BF16)
    dev = 0.5 * (sd + pltpu.roll(sd, WIDTH - 1, 0))
    here = pl.ds(pl.multiple_of(r * WIDTH, WIDTH), WIDTH)
    hi_scr[here, :] = dev.astype(BF16)
    mw = jnp.broadcast_to(ms, (WIDTH, 128))
    pm = 0.5 * (mw + pltpu.roll(mw, WIDTH - 1, 0))
    p0, rest = halves(pm)
    p1, p2 = halves(rest)
    lane = lax.broadcasted_iota(jnp.int32, (WIDTH, 128), 1)
    m_scr[here, :] = jnp.where(
        lane == 0, p0, jnp.where(lane == 1, p1, jnp.where(lane == 2, p2, 0.0))
    ).astype(BF16)

    @pl.when(r == ROWS - 1)
    def _():
        local = pos_ref[0:1, :] - row0_ref[0]
        col = pos_ref[1:2, :]
        left = (col + side_ref[...] - 1) & (WIDTH - 1)
        index = column((local * WIDTH + left).astype(F32)).astype(jnp.int32)
        cells = lax.broadcasted_iota(jnp.int32, (OBS, CELLS), 1)
        pick = jnp.where(cells == index, 1.0, 0.0).astype(BF16)
        square = jnp.zeros((OBS, 128), F32)
        for b in range(4):
            part = slice(b * 256, (b + 1) * 256)
            a = jnp.dot(pick, hi_scr[:, part], preferred_element_type=F32)
            a_ref[0:OBS, part] = a.astype(BF16)
            square = square + a[:, 0:128] * a[:, 0:128] + a[:, 128:256] * a[:, 128:256]
        mean = jnp.dot(pick, m_scr[...], preferred_element_type=F32)
        lane_o = lax.broadcasted_iota(jnp.int32, (OBS, 128), 1)
        both = jnp.where(
            lane_o == 0,
            jnp.sum(mean, axis=1, keepdims=True),
            jnp.sum(square, axis=1, keepdims=True),
        ).T
        sigma = sigma_ref[...]
        scale = 1.0 / (both[1:2, :] * (1.0 / (M - 1)) + sigma * sigma)
        lines = [local.astype(F32), col.astype(F32)]
        for v in (value_ref[...] - both[0:1, :], sigma, scale):
            lines.extend(halves(v))
        sub = lax.broadcasted_iota(jnp.int32, (16, OBS), 0)
        code = jnp.zeros((16, OBS), F32)
        for i, line in enumerate(lines):
            code = jnp.where(sub == i, line, code)
        a_ref[OBS : OBS + 16, 0:OBS] = code.astype(BF16)
        a_ref[OBS : OBS + 16, OBS:M] = jnp.zeros((16, M - OBS), BF16)


def anomalies(row0, state, pos, side, value, sigma):
    full = lambda shape: pl.BlockSpec(shape, lambda r: (0,) * len(shape))
    tile = pl.BlockSpec((WIDTH, M), lambda r: (r, 0))
    return pl.pallas_call(
        anomaly_kernel,
        grid=(ROWS,),
        in_specs=[pl.BlockSpec(memory_space=pltpu.SMEM), tile, full((2, OBS))]
        + [full((1, OBS))] * 3,
        out_specs=[tile, full((OBS + 16, M))],
        out_shape=[
            jax.ShapeDtypeStruct((CELLS, M), BF16),
            jax.ShapeDtypeStruct((OBS + 16, M), BF16),
        ],
        scratch_shapes=[pltpu.VMEM((CELLS, M), BF16), pltpu.VMEM((CELLS, 128), BF16)],
        compiler_params=pltpu.CompilerParams(
            vmem_limit_bytes=PREP_VMEM, dimension_semantics=("arbitrary",)
        ),
        cost_estimate=cost(1 << 20, 1 << 16),
        name="anomalies",
    )(row0, state, pos, side, value, sigma)


def weights(a_ref, n_ref, w_ref):
    code = a_ref[OBS : OBS + 16, 0:OBS].astype(F32).T
    base = code[:, 2:3] + code[:, 3:4]
    sigma = code[:, 4:5] + code[:, 5:6]
    scale = code[:, 6:7] + code[:, 7:8]
    for i in range(OBS // 32):
        rows = slice(i * 32, (i + 1) * 32)
        w = base[rows] + sigma[rows] * n_ref[rows, :].astype(F32) - a_ref[rows, :].astype(F32)
        w_ref[rows, :] = (w * scale[rows]).astype(BF16)


def covariance(x, a_ref, cov_ref):
    cov_ref[...] = lax.dot_general(
        x, a_ref[0:OBS, :], (((1,), (1,)), ((), ())), preferred_element_type=F32
    )


def gain_rows(r, a_ref, offset, cov_ref, g_ref):
    code = a_ref[OBS : OBS + 16, 0:OBS].astype(F32)
    gap = jnp.abs(code[0:1, :] + (ROWS * offset - r).astype(F32))
    row2 = jnp.where(gap > REACH * ROWS, 1e4, jnp.maximum(gap * gap * (1.0 / 256.0), 1e-12))
    col = code[1:2, :] * (1.0 / 16.0)
    n1 = 1.0 / (M - 1)
    for i in range(WIDTH // CHUNK):
        rows = slice(i * CHUNK, (i + 1) * CHUNK)
        q = (lax.broadcasted_iota(jnp.int32, (CHUNK, 1), 0) + i * CHUNK).astype(F32) * (1.0 / 16.0)
        d = jnp.abs(q - col)
        d = jnp.minimum(d, 16.0 - d)
        z2 = d * d + row2
        inv = lax.rsqrt(z2)
        z = z2 * inv
        near = z2 * (z * ((0.625 * n1) + z * ((0.5 * n1) - (0.25 * n1) * z)) - (5.0 / 3.0 * n1)) + n1
        u = jnp.maximum(2.0 - z, 0.0)
        u2 = u * u
        far = (u2 * u2) * ((z2 + (2.0 * z - 0.5)) * (inv * (n1 / 12.0)))
        g_ref[rows, :] = (jnp.where(z2 <= 1.0, near, far) * cov_ref[rows, :]).astype(BF16)


def in_vmem():
    return pl.BlockSpec(memory_space=pltpu.VMEM)


def in_smem():
    return pl.BlockSpec(memory_space=pltpu.SMEM)


def contribute_kernel(distances, sign_ref, x_ref, *refs):
    n = len(distances)
    a_refs = refs[0:n]
    n_refs = refs[n : 2 * n]
    add_refs = refs[2 * n : -4]
    out_ref, cov_scr, g_scr, w_scr = refs[-4:]
    for k in range(n):
        weights(a_refs[k], n_refs[k], w_scr.at[k])

    @pl.loop(0, ROWS)
    def _(r):
        here = pl.ds(pl.multiple_of(r * WIDTH, WIDTH), WIDTH)
        for k in range(n):
            covariance(x_ref[here, :], a_refs[k], cov_scr.at[k])
        for k, distance in enumerate(distances):
            gain_rows(r, a_refs[k], sign_ref[0] * distance, cov_scr.at[k], g_scr.at[k])
        for h in range(2):
            part = slice(h * (M // 2), (h + 1) * (M // 2))
            terms = [ref[here, part] for ref in add_refs]
            for k in range(n):
                terms.append(
                    jnp.dot(g_scr[k], w_scr[k, :, part], preferred_element_type=F32)
                )
            out_ref[here, part] = functools.reduce(jnp.add, terms)


def contribute(sign, x, packets, distances, *add):
    n = len(distances)
    return pl.pallas_call(
        functools.partial(contribute_kernel, distances),
        in_specs=[in_smem()] + [in_vmem()] * (2 * n + 1 + len(add)),
        out_specs=in_vmem(),
        out_shape=jax.ShapeDtypeStruct((CELLS, M), F32),
        scratch_shapes=[
            pltpu.VMEM((n, WIDTH, OBS), F32),
            pltpu.VMEM((n, WIDTH, OBS), BF16),
            pltpu.VMEM((n, OBS, M), BF16),
        ],
        input_output_aliases={2 + 2 * n: 0} if add else {},
        compiler_params=params(),
        cost_estimate=cost(1 << 20, 1 << 16),
        name="contribute",
    )(sign, x, *[a for a, _ in packets], *[n for _, n in packets], *add)


def gain_kernel(distance, sign_ref, x_ref, a_ref, g_ref, cov_scr):
    @pl.loop(0, ROWS)
    def _(r):
        here = pl.ds(pl.multiple_of(r * WIDTH, WIDTH), WIDTH)
        covariance(x_ref[here, :], a_ref, cov_scr)
        gain_rows(r, a_ref, sign_ref[0] * distance, cov_scr, g_ref.at[here])


def gains(sign, x, a, distance):
    return pl.pallas_call(
        functools.partial(gain_kernel, distance),
        in_specs=[in_smem(), in_vmem(), in_vmem()],
        out_specs=in_vmem(),
        out_shape=jax.ShapeDtypeStruct((CELLS, OBS), BF16),
        scratch_shapes=[pltpu.VMEM((WIDTH, OBS), F32)],
        compiler_params=params(),
        cost_estimate=cost(1 << 20, 1 << 16),
        name="gains",
    )(sign, x, a)


def edge_kernel(sign_ref, acc_ref, g_ref, a_ref, n_ref, out_ref, cross_ref, inner_ref, w_ref):
    weights(a_ref, n_ref, w_ref)
    for i in range(2):
        here = slice(3 * i * WIDTH, (3 * i + 1) * WIDTH)
        for h in range(4):
            part = slice(h * (M // 4), (h + 1) * (M // 4))
            total = acc_ref[here, part] + jnp.dot(
                g_ref[here, :], w_ref[:, part], preferred_element_type=F32
            )
            out_ref[here, part] = total
            outward = 2 * i - 1 == sign_ref[0]

            @pl.when(jnp.logical_not(outward))
            def _():
                inner_ref[:, part] = total.astype(BF16)

            @pl.when(outward)
            def _():
                cross_ref[:, part] = total.astype(BF16)


def edges(sign, acc, gain, a, noise):
    return pl.pallas_call(
        edge_kernel,
        in_specs=[in_smem()] + [in_vmem()] * 4,
        out_specs=[in_vmem()] * 4,
        out_shape=[
            jax.ShapeDtypeStruct((CELLS, M), F32),
            jax.ShapeDtypeStruct((WIDTH, M), BF16),
            jax.ShapeDtypeStruct((WIDTH, M), BF16),
            jax.ShapeDtypeStruct((OBS, M), BF16),
        ],
        input_output_aliases={1: 0},
        compiler_params=params(),
        cost_estimate=cost(1 << 20, 1 << 16),
        name="edges",
    )(sign, acc, gain, a, noise)


def advance(a, above, below):
    right = pltpu.roll(a, WIDTH - 1, 0)
    left = pltpu.roll(a, 1, 0)
    pull = 0.05 * a * (above - below + (right - left))
    spread = 0.2 * (above + below + right + left - 4.0 * a)
    return a - pull + spread


def middle_kernel(acc_ref, g_ref, w_ref, mid_ref, out_ref, pred_scr, sems):
    rows = lambda r: slice(r * WIDTH, (r + 1) * WIDTH)
    copies = []
    for h in range(4):
        part = slice(h * (M // 4), (h + 1) * (M // 4))
        mids = []
        for i in range(2):
            total = acc_ref[rows(1 + i), part] + jnp.dot(
                g_ref[rows(1 + i), :], w_ref[:, part], preferred_element_type=F32
            )
            mid_ref[rows(i), part] = total
            mids.append(total)
        pred_scr[rows(0), part] = advance(mids[0], mids[1], acc_ref[rows(0), part])
        pred_scr[rows(1), part] = advance(mids[1], acc_ref[rows(3), part], mids[0])
        copies.append(
            pltpu.make_async_copy(
                pred_scr.at[:, part], out_ref.at[WIDTH : 3 * WIDTH, part], sems.at[h]
            )
        )
        copies[-1].start()
    for copy in copies:
        copy.wait()


def middle(acc, gain, w):
    return pl.pallas_call(
        middle_kernel,
        in_specs=[in_vmem()] * 3,
        out_specs=[in_vmem(), pl.BlockSpec(memory_space=pl.ANY)],
        out_shape=[
            jax.ShapeDtypeStruct((2 * WIDTH, M), F32),
            jax.ShapeDtypeStruct((CELLS, M), F32),
        ],
        scratch_shapes=[pltpu.VMEM((2 * WIDTH, M), F32), pltpu.SemaphoreType.DMA((4,))],
        compiler_params=params(),
        cost_estimate=cost(1 << 20, 1 << 16),
        name="middle",
    )(acc, gain, w)


def outer_kernel(sign_ref, acc_ref, mid_ref, cross_ref, inner_ref, _, out_ref, pred_scr, sems):
    rows = lambda r: slice(r * WIDTH, (r + 1) * WIDTH)
    first = sign_ref[0] < 0
    copies = []
    for h in range(4):
        part = slice(h * (M // 4), (h + 1) * (M // 4))
        cross = cross_ref[:, part].astype(F32)
        inner = inner_ref[:, part].astype(F32)
        before = jnp.where(first, cross, inner)
        after = jnp.where(first, inner, cross)
        pred_scr[rows(0), part] = advance(acc_ref[rows(0), part], mid_ref[rows(0), part], before)
        pred_scr[rows(1), part] = advance(acc_ref[rows(3), part], after, mid_ref[rows(1), part])
        for i in range(2):
            copies.append(
                pltpu.make_async_copy(
                    pred_scr.at[rows(i), part], out_ref.at[rows(3 * i), part], sems.at[2 * h + i]
                )
            )
            copies[-1].start()
    for copy in copies:
        copy.wait()


def outer(sign, acc, mid, cross, inner, out):
    return pl.pallas_call(
        outer_kernel,
        in_specs=[in_smem()] + [in_vmem()] * 4 + [pl.BlockSpec(memory_space=pl.ANY)],
        out_specs=pl.BlockSpec(memory_space=pl.ANY),
        out_shape=jax.ShapeDtypeStruct((CELLS, M), F32),
        scratch_shapes=[pltpu.VMEM((2 * WIDTH, M), F32), pltpu.SemaphoreType.DMA((8,))],
        input_output_aliases={5: 0},
        compiler_params=params(),
        cost_estimate=cost(1 << 20, 1 << 16),
        name="outer",
    )(sign, acc, mid, cross, inner, out)


def hold(value, acc):
    held, acc = lax.optimization_barrier((value, acc))
    return held, acc


def on_device(state, obs_value, obs_sigma, obs_noise, obs_pos, obs_side):
    device = lax.axis_index("space")
    slabs = lax.axis_size("space")
    pairs = [(i, i ^ 1) for i in range(slabs)]
    across = [(i, (i + 1 if i % 2 else i - 1) % slabs) for i in range(slabs)]
    inside = lambda block: lax.ppermute(block, "space", pairs)
    beyond = lambda block: lax.ppermute(block, "space", across)
    row0 = (device * ROWS).astype(jnp.int32).reshape(1)
    sign = (2 * (device % 2) - 1).astype(jnp.int32).reshape(1)
    row = lambda v: v.reshape(1, OBS)
    own_n, held = lax.optimization_barrier((obs_noise.astype(BF16), state))
    x, own_a = anomalies(
        row0, held, obs_pos, row(obs_side), row(obs_value), row(obs_sigma)
    )

    one_n, one_a = beyond(own_n), beyond(own_a)
    twin_n, twin_a = inside(own_n), inside(own_a)
    two_a, two_n = beyond(twin_a), beyond(twin_n)
    acc = contribute(sign, x, ((own_a, own_n), (twin_a, twin_n)), (0, -1))
    one_twin_n = inside(one_n)
    one_a, acc, one_twin_n = lax.optimization_barrier((one_a, acc, one_twin_n))
    one_twin_a = inside(one_a)
    one_twin_a, two_a = hold(one_twin_a, two_a)
    three_a, three_n = beyond(one_twin_a), beyond(one_twin_n)
    acc = contribute(sign, x, ((one_a, one_n), (one_twin_a, one_twin_n)), (1, -2), acc, state)
    two_n, acc = hold(two_n, acc)
    two_twin_a, two_twin_n = inside(two_a), inside(two_n)
    two_twin_a, three_a = hold(two_twin_a, three_a)
    four_a, four_n = beyond(two_twin_a), beyond(two_twin_n)
    acc = contribute(sign, x, ((two_a, two_n), (two_twin_a, two_twin_n)), (2, -3), acc)
    three_n, acc = hold(three_n, acc)
    three_twin_a, three_twin_n = inside(three_a), inside(three_n)
    acc = contribute(sign, x, ((three_a, three_n), (three_twin_a, three_twin_n)), (3, -4), acc)
    four_a, acc = hold(four_a, acc)
    gain = gains(sign, x, four_a, 4)
    acc, to_cross, to_inner, four_w = edges(sign, acc, gain, four_a, four_n)
    cross, inner = beyond(to_cross), inside(to_inner)
    mid, out = middle(acc, gain, four_w)
    return outer(sign, acc, mid, cross, inner, out)


def solution(mesh):
    placed = (
        P("space", None),
        P("space"),
        P("space"),
        P("space", None),
        P(None, "space"),
        P("space"),
    )
    return jax.shard_map(
        on_device, mesh=mesh, in_specs=placed, out_specs=P("space", None), check_vma=False
    )
```

```python
import functools

import jax
import jax.numpy as jnp
from jax import lax
from jax.experimental import pallas as pl
from jax.experimental.pallas import tpu as pltpu
from jax.sharding import PartitionSpec as P

WIDTH = 256
ROWS = 4
REACH = 4
CELLS = ROWS * WIDTH
OBS = 512
M = 1024
CHUNK = 16
LANES = M // 2
PREP_VMEM = 61 * 1024 * 1024
VMEM = 20 * 1024 * 1024
F32 = jnp.float32
BF16 = jnp.bfloat16


def params():
    return pltpu.CompilerParams(vmem_limit_bytes=VMEM)


def cost(flops, nbytes):
    return pl.CostEstimate(flops=int(flops), bytes_accessed=int(nbytes), transcendentals=0)


def column(row):
    return jnp.broadcast_to(row, (8, row.shape[1])).T[:, 0:1]


def halves(v):
    high = v.astype(BF16).astype(F32)
    return high, v - high


def anomaly_kernel(
    row0_ref, state_ref, pos_ref, side_ref, value_ref, sigma_ref, x_ref, a_ref, hi_scr, m_scr
):
    r = pl.program_id(0)
    s = state_ref[...]
    ms = jnp.mean(s, axis=1, keepdims=True)
    sd = s - ms
    x_ref[...] = sd.astype(BF16)
    dev = 0.5 * (sd + pltpu.roll(sd, WIDTH - 1, 0))
    here = pl.ds(pl.multiple_of(r * WIDTH, WIDTH), WIDTH)
    hi_scr[here, :] = dev.astype(BF16)
    mw = jnp.broadcast_to(ms, (WIDTH, 128))
    pm = 0.5 * (mw + pltpu.roll(mw, WIDTH - 1, 0))
    p0, rest = halves(pm)
    p1, p2 = halves(rest)
    lane = lax.broadcasted_iota(jnp.int32, (WIDTH, 128), 1)
    m_scr[here, :] = jnp.where(
        lane == 0, p0, jnp.where(lane == 1, p1, jnp.where(lane == 2, p2, 0.0))
    ).astype(BF16)

    @pl.when(r == ROWS - 1)
    def _():
        local = pos_ref[0:1, :] - row0_ref[0]
        col = pos_ref[1:2, :]
        left = (col + side_ref[...] - 1) & (WIDTH - 1)
        index = column((local * WIDTH + left).astype(F32)).astype(jnp.int32)
        cells = lax.broadcasted_iota(jnp.int32, (OBS, CELLS), 1)
        pick = jnp.where(cells == index, 1.0, 0.0).astype(BF16)
        square = jnp.zeros((OBS, 128), F32)
        for b in range(4):
            part = slice(b * 256, (b + 1) * 256)
            a = jnp.dot(pick, hi_scr[:, part], preferred_element_type=F32)
            a_ref[0:OBS, part] = a.astype(BF16)
            square = square + a[:, 0:128] * a[:, 0:128] + a[:, 128:256] * a[:, 128:256]
        mean = jnp.dot(pick, m_scr[...], preferred_element_type=F32)
        lane_o = lax.broadcasted_iota(jnp.int32, (OBS, 128), 1)
        both = jnp.where(
            lane_o == 0,
            jnp.sum(mean, axis=1, keepdims=True),
            jnp.sum(square, axis=1, keepdims=True),
        ).T
        sigma = sigma_ref[...]
        scale = 1.0 / (both[1:2, :] * (1.0 / (M - 1)) + sigma * sigma)
        lines = [local.astype(F32), col.astype(F32)]
        for v in (value_ref[...] - both[0:1, :], sigma, scale):
            lines.extend(halves(v))
        sub = lax.broadcasted_iota(jnp.int32, (16, OBS), 0)
        code = jnp.zeros((16, OBS), F32)
        for i, line in enumerate(lines):
            code = jnp.where(sub == i, line, code)
        a_ref[OBS : OBS + 16, 0:OBS] = code.astype(BF16)
        a_ref[OBS : OBS + 16, OBS:M] = jnp.zeros((16, M - OBS), BF16)


def anomalies(row0, state, pos, side, value, sigma):
    full = lambda shape: pl.BlockSpec(shape, lambda r: (0,) * len(shape))
    tile = pl.BlockSpec((WIDTH, M), lambda r: (r, 0))
    return pl.pallas_call(
        anomaly_kernel,
        grid=(ROWS,),
        in_specs=[pl.BlockSpec(memory_space=pltpu.SMEM), tile, full((2, OBS))]
        + [full((1, OBS))] * 3,
        out_specs=[tile, full((OBS + 16, M))],
        out_shape=[
            jax.ShapeDtypeStruct((CELLS, M), BF16),
            jax.ShapeDtypeStruct((OBS + 16, M), BF16),
        ],
        scratch_shapes=[pltpu.VMEM((CELLS, M), BF16), pltpu.VMEM((CELLS, 128), BF16)],
        compiler_params=pltpu.CompilerParams(
            vmem_limit_bytes=PREP_VMEM, dimension_semantics=("arbitrary",)
        ),
        cost_estimate=cost(1 << 20, 1 << 16),
        name="anomalies",
    )(row0, state, pos, side, value, sigma)


def weights(a_ref, n_refs, w_ref):
    code = a_ref[OBS : OBS + 16, 0:OBS].astype(F32).T
    base = code[:, 2:3] + code[:, 3:4]
    sigma = code[:, 4:5] + code[:, 5:6]
    scale = code[:, 6:7] + code[:, 7:8]
    for h, n_ref in n_refs:
        part = slice(h * n_ref.shape[1], (h + 1) * n_ref.shape[1])
        to = part if w_ref.shape[1] == M else slice(0, n_ref.shape[1])
        for i in range(OBS // 32):
            rows = slice(i * 32, (i + 1) * 32)
            w = base[rows] + sigma[rows] * n_ref[rows, :].astype(F32)
            w = w - a_ref[rows, part].astype(F32)
            w_ref[rows, to] = (w * scale[rows]).astype(BF16)


def covariance(x, a_ref, cov_ref):
    for h in range(2):
        part = slice(h * 256, (h + 1) * 256)
        cov_ref[:, part] = lax.dot_general(
            x, a_ref[part, :], (((1,), (1,)), ((), ())), preferred_element_type=F32
        )


def gain_rows(a_ref, offset, cov_ref, g_ref, unroll=4):
    code = a_ref[OBS : OBS + 16, 0:OBS].astype(F32)
    col = code[1:2, :] * (1.0 / 16.0)
    n1 = 1.0 / (M - 1)
    row2 = []
    for r in range(ROWS):
        gap = jnp.abs(code[0:1, :] + (ROWS * offset - r).astype(F32))
        row2.append(
            jnp.where(gap > REACH * ROWS, 1e4, jnp.maximum(gap * gap * (1.0 / 256.0), 1e-12))
        )

    @pl.loop(0, WIDTH // CHUNK, unroll=unroll)
    def _(i):
        q = lax.broadcasted_iota(jnp.int32, (CHUNK, 1), 0) + i * CHUNK
        q = q.astype(F32) * (1.0 / 16.0)
        for h in range(2):
            part = slice(h * 256, (h + 1) * 256)
            d = jnp.abs(q - col[:, part])
            d = jnp.minimum(d, 16.0 - d)
            d = d * d
            for r in range(ROWS):
                rows = pl.ds(pl.multiple_of(r * WIDTH + i * CHUNK, CHUNK), CHUNK)
                z2 = d + row2[r][:, part]
                inv = lax.rsqrt(z2)
                z = z2 * inv
                near = (
                    z2 * (z * ((0.625 * n1) + z * ((0.5 * n1) - (0.25 * n1) * z)) - (5.0 / 3.0 * n1))
                    + n1
                )
                u = jnp.maximum(2.0 - z, 0.0)
                u2 = u * u
                far = (u2 * u2) * ((z2 + (2.0 * z - 0.5)) * (inv * (n1 / 12.0)))
                g_ref[rows, part] = (
                    jnp.where(z2 <= 1.0, near, far) * cov_ref[rows, part]
                ).astype(BF16)


def in_vmem():
    return pl.BlockSpec(memory_space=pltpu.VMEM)


def in_smem():
    return pl.BlockSpec(memory_space=pltpu.SMEM)


def contribute_kernel(distances, counts, unroll, sign_ref, x_ref, *refs):
    n = len(distances)
    a_refs = refs[0:n]
    refs = refs[n:]
    out_ref, cov_scr, g_scr, w_scr = refs[-4:]
    for k in range(n):
        weights(a_refs[k], list(enumerate(refs[0 : counts[k]])), w_scr.at[k])
        refs = refs[counts[k] :]
    add_refs = refs[:-4]
    for k, distance in enumerate(distances):
        covariance(x_ref[...], a_refs[k], cov_scr.at[k])
    for k, distance in enumerate(distances):
        gain_rows(a_refs[k], sign_ref[0] * distance, cov_scr.at[k], g_scr.at[k], unroll)
    for h in range(4):
        part = slice(h * (M // 4), (h + 1) * (M // 4))
        terms = [ref[:, part] for ref in add_refs]
        for k in range(n):
            terms.append(jnp.dot(g_scr[k], w_scr[k, :, part], preferred_element_type=F32))
        out_ref[:, part] = functools.reduce(jnp.add, terms)


def contribute(sign, x, packets, distances, *add, unroll=4):
    n = len(distances)
    blocks = [a for a, _ in packets]
    for _, parts in packets:
        blocks.extend(parts)
    return pl.pallas_call(
        functools.partial(
            contribute_kernel, distances, [len(parts) for _, parts in packets], unroll
        ),
        in_specs=[in_smem()] + [in_vmem()] * (1 + len(blocks) + len(add)),
        out_specs=in_vmem(),
        out_shape=jax.ShapeDtypeStruct((CELLS, M), F32),
        scratch_shapes=[
            pltpu.VMEM((n, CELLS, OBS), F32),
            pltpu.VMEM((n, CELLS, OBS), BF16),
            pltpu.VMEM((n, OBS, M), BF16),
        ],
        input_output_aliases={2 + len(blocks): 0} if add else {},
        compiler_params=params(),
        cost_estimate=cost(1 << 20, 1 << 16),
        name="contribute",
    )(sign, x, *blocks, *add)


def gain_kernel(distance, sign_ref, x_ref, a_ref, g_ref, cov_scr):
    covariance(x_ref[...], a_ref, cov_scr)
    gain_rows(a_ref, sign_ref[0] * distance, cov_scr, g_ref, 16)


def gains(sign, x, a, distance):
    return pl.pallas_call(
        functools.partial(gain_kernel, distance),
        in_specs=[in_smem(), in_vmem(), in_vmem()],
        out_specs=in_vmem(),
        out_shape=jax.ShapeDtypeStruct((CELLS, OBS), BF16),
        scratch_shapes=[pltpu.VMEM((CELLS, OBS), F32)],
        compiler_params=params(),
        cost_estimate=cost(1 << 20, 1 << 16),
        name="gains",
    )(sign, x, a)


def edge_kernel(half, sign_ref, acc_ref, g_ref, a_ref, n_ref, out_ref, cross_ref, inner_ref, w_ref):
    weights(a_ref, [(half, n_ref)], w_ref)
    for i in range(2):
        here = slice(3 * i * WIDTH, (3 * i + 1) * WIDTH)
        outward = 2 * i - 1 == sign_ref[0]
        for h in range(2):
            part = slice(h * 256, (h + 1) * 256)
            total = acc_ref[here, half * LANES + h * 256 : half * LANES + (h + 1) * 256]
            total = total + jnp.dot(g_ref[here, :], w_ref[:, part], preferred_element_type=F32)
            out_ref[i * WIDTH : (i + 1) * WIDTH, part] = total

            @pl.when(jnp.logical_not(outward))
            def _():
                inner_ref[:, part] = total.astype(BF16)

            @pl.when(outward)
            def _():
                cross_ref[:, part] = total.astype(BF16)


def edges(sign, acc, gain, a, noise, half):
    return pl.pallas_call(
        functools.partial(edge_kernel, half),
        in_specs=[in_smem()] + [in_vmem()] * 4,
        out_specs=[in_vmem()] * 4,
        out_shape=[
            jax.ShapeDtypeStruct((2 * WIDTH, LANES), F32),
            jax.ShapeDtypeStruct((WIDTH, LANES), BF16),
            jax.ShapeDtypeStruct((WIDTH, LANES), BF16),
            jax.ShapeDtypeStruct((OBS, LANES), BF16),
        ],
        compiler_params=params(),
        cost_estimate=cost(1 << 20, 1 << 16),
        name="edges",
    )(sign, acc, gain, a, noise)


def advance(a, above, below):
    right = pltpu.roll(a, WIDTH - 1, 0)
    left = pltpu.roll(a, 1, 0)
    pull = 0.05 * a * (above - below + (right - left))
    spread = 0.2 * (above + below + right + left - 4.0 * a)
    return a - pull + spread


def middle_kernel(half, acc_ref, g_ref, w_ref, edge_ref, *refs):
    mid_ref, out_ref, pred_scr, sems = refs[-4:]
    rows = lambda r: slice(r * WIDTH, (r + 1) * WIDTH)
    copies = []
    for h in range(2):
        part = slice(h * 256, (h + 1) * 256)
        far = slice(half * LANES + h * 256, half * LANES + (h + 1) * 256)
        mids = []
        for i in range(2):
            total = acc_ref[rows(1 + i), far] + jnp.dot(
                g_ref[rows(1 + i), :], w_ref[:, part], preferred_element_type=F32
            )
            mid_ref[rows(i), part] = total
            mids.append(total)
        pred_scr[rows(0), part] = advance(mids[0], mids[1], edge_ref[rows(0), part])
        pred_scr[rows(1), part] = advance(mids[1], edge_ref[rows(1), part], mids[0])
        copies.append(
            pltpu.make_async_copy(
                pred_scr.at[:, part], out_ref.at[WIDTH : 3 * WIDTH, far], sems.at[h]
            )
        )
        copies[-1].start()
    for copy in copies:
        copy.wait()


def middle(acc, gain, w, edge, half, *out):
    return pl.pallas_call(
        functools.partial(middle_kernel, half),
        in_specs=[in_vmem()] * 4 + [pl.BlockSpec(memory_space=pl.ANY)] * len(out),
        out_specs=[in_vmem(), pl.BlockSpec(memory_space=pl.ANY)],
        out_shape=[
            jax.ShapeDtypeStruct((2 * WIDTH, LANES), F32),
            jax.ShapeDtypeStruct((CELLS, M), F32),
        ],
        scratch_shapes=[pltpu.VMEM((2 * WIDTH, LANES), F32), pltpu.SemaphoreType.DMA((2,))],
        input_output_aliases={4: 1} if out else {},
        compiler_params=params(),
        cost_estimate=cost(1 << 20, 1 << 16),
        name="middle",
    )(acc, gain, w, edge, *out)


def outer_kernel(
    half, sign_ref, edge_ref, mid_ref, cross_ref, inner_ref, _, out_ref, pred_scr, sems
):
    rows = lambda r: slice(r * WIDTH, (r + 1) * WIDTH)
    first = sign_ref[0] < 0
    copies = []
    for h in range(2):
        part = slice(h * 256, (h + 1) * 256)
        far = slice(half * LANES + h * 256, half * LANES + (h + 1) * 256)
        cross = cross_ref[:, part].astype(F32)
        inner = inner_ref[:, part].astype(F32)
        before = jnp.where(first, cross, inner)
        after = jnp.where(first, inner, cross)
        pred_scr[rows(0), part] = advance(edge_ref[rows(0), part], mid_ref[rows(0), part], before)
        pred_scr[rows(1), part] = advance(edge_ref[rows(1), part], after, mid_ref[rows(1), part])
        for i in range(2):
            copies.append(
                pltpu.make_async_copy(
                    pred_scr.at[rows(i), part], out_ref.at[rows(3 * i), far], sems.at[2 * h + i]
                )
            )
            copies[-1].start()
    for copy in copies:
        copy.wait()


def outer(sign, edge, mid, cross, inner, half, out):
    return pl.pallas_call(
        functools.partial(outer_kernel, half),
        in_specs=[in_smem()] + [in_vmem()] * 4 + [pl.BlockSpec(memory_space=pl.ANY)],
        out_specs=pl.BlockSpec(memory_space=pl.ANY),
        out_shape=jax.ShapeDtypeStruct((CELLS, M), F32),
        scratch_shapes=[pltpu.VMEM((2 * WIDTH, LANES), F32), pltpu.SemaphoreType.DMA((4,))],
        input_output_aliases={5: 0},
        compiler_params=params(),
        cost_estimate=cost(1 << 20, 1 << 16),
        name="outer",
    )(sign, edge, mid, cross, inner, out)


def hold(value, acc):
    held, acc = lax.optimization_barrier((value, acc))
    return held, acc


def on_device(state, obs_value, obs_sigma, obs_noise, obs_pos, obs_side):
    device = lax.axis_index("space")
    slabs = lax.axis_size("space")
    pairs = [(i, i ^ 1) for i in range(slabs)]
    across = [(i, (i + 1 if i % 2 else i - 1) % slabs) for i in range(slabs)]
    inside = lambda block: lax.ppermute(block, "space", pairs)
    beyond = lambda block: lax.ppermute(block, "space", across)
    row0 = (device * ROWS).astype(jnp.int32).reshape(1)
    sign = (2 * (device % 2) - 1).astype(jnp.int32).reshape(1)
    row = lambda v: v.reshape(1, OBS)
    own_n, held = lax.optimization_barrier((obs_noise.astype(BF16), state))
    x, own_a = anomalies(
        row0, held, obs_pos, row(obs_side), row(obs_value), row(obs_sigma)
    )

    one_n, one_a = beyond(own_n), beyond(own_a)
    twin_n, twin_a = inside(own_n), inside(own_a)
    two_a, two_n = beyond(twin_a), beyond(twin_n)
    acc = contribute(sign, x, ((own_a, (own_n,)), (twin_a, (twin_n,))), (0, -1))
    one_twin_n = inside(one_n)
    one_a, acc, one_twin_n = lax.optimization_barrier((one_a, acc, one_twin_n))
    one_twin_a = inside(one_a)
    one_twin_a, two_a = hold(one_twin_a, two_a)
    three_a, three_n = beyond(one_twin_a), beyond(one_twin_n)
    acc = contribute(sign, x, ((one_a, (one_n,)), (one_twin_a, (one_twin_n,))), (1, -2), acc, state)
    two_n, acc = hold(two_n, acc)
    two_twin_a = inside(two_a)
    two_twin_n = [inside(two_n[:, h * LANES : (h + 1) * LANES]) for h in range(2)]
    two_twin_a, three_a = hold(two_twin_a, three_a)
    four_a, four_n = beyond(two_twin_a), [beyond(n) for n in two_twin_n]
    acc = contribute(sign, x, ((two_a, (two_n,)), (two_twin_a, two_twin_n)), (2, -3), acc)
    three_n, acc = hold(three_n, acc)
    three_twin_a, three_twin_n = inside(three_a), inside(three_n)
    last = ((three_a, (three_n,)), (three_twin_a, (three_twin_n,)))
    acc = contribute(sign, x, last, (3, -4), acc, unroll=16)
    four_a, acc = hold(four_a, acc)
    gain = gains(sign, x, four_a, 4)
    done = []
    out = ()
    for half in range(2):
        edge, to_cross, to_inner, w = edges(sign, acc, gain, four_a, four_n[half], half)
        cross, inner = beyond(to_cross), inside(to_inner)
        mid, *out = middle(acc, gain, w, edge, half, *out)
        done.append((edge, mid, cross, inner))
    out = out[0]
    for half in range(2):
        out = outer(sign, *done[half], half, out)
    return out


def solution(mesh):
    placed = (
        P("space", None),
        P("space"),
        P("space"),
        P("space", None),
        P(None, "space"),
        P("space"),
    )
    return jax.shard_map(
        on_device, mesh=mesh, in_specs=placed, out_specs=P("space", None), check_vma=False
    )
```

```python
import functools

import jax
import jax.numpy as jnp
from jax import lax
from jax.experimental import pallas as pl
from jax.experimental.pallas import tpu as pltpu
from jax.sharding import PartitionSpec as P

WIDTH = 256
ROWS = 4
REACH = 4
CELLS = ROWS * WIDTH
OBS = 512
M = 1024
CHUNK = 16
PREP_VMEM = 61 * 1024 * 1024
VMEM = 20 * 1024 * 1024
F32 = jnp.float32
BF16 = jnp.bfloat16


def params():
    return pltpu.CompilerParams(vmem_limit_bytes=VMEM)


def cost(flops, nbytes):
    return pl.CostEstimate(flops=int(flops), bytes_accessed=int(nbytes), transcendentals=0)


def column(row):
    return jnp.broadcast_to(row, (8, row.shape[1])).T[:, 0:1]


def halves(v):
    high = v.astype(BF16).astype(F32)
    return high, v - high


def anomaly_kernel(
    row0_ref, state_ref, pos_ref, side_ref, value_ref, sigma_ref, x_ref, a_ref, hi_scr, m_scr
):
    r = pl.program_id(0)
    s = state_ref[...]
    ms = jnp.mean(s, axis=1, keepdims=True)
    sd = s - ms
    x_ref[...] = sd.astype(BF16)
    dev = 0.5 * (sd + pltpu.roll(sd, WIDTH - 1, 0))
    here = pl.ds(pl.multiple_of(r * WIDTH, WIDTH), WIDTH)
    hi_scr[here, :] = dev.astype(BF16)
    mw = jnp.broadcast_to(ms, (WIDTH, 128))
    pm = 0.5 * (mw + pltpu.roll(mw, WIDTH - 1, 0))
    p0, rest = halves(pm)
    p1, p2 = halves(rest)
    lane = lax.broadcasted_iota(jnp.int32, (WIDTH, 128), 1)
    m_scr[here, :] = jnp.where(
        lane == 0, p0, jnp.where(lane == 1, p1, jnp.where(lane == 2, p2, 0.0))
    ).astype(BF16)

    @pl.when(r == ROWS - 1)
    def _():
        local = pos_ref[0:1, :] - row0_ref[0]
        col = pos_ref[1:2, :]
        left = (col + side_ref[...] - 1) & (WIDTH - 1)
        index = column((local * WIDTH + left).astype(F32)).astype(jnp.int32)
        cells = lax.broadcasted_iota(jnp.int32, (OBS, CELLS), 1)
        pick = jnp.where(cells == index, 1.0, 0.0).astype(BF16)
        square = jnp.zeros((OBS, 128), F32)
        for b in range(4):
            part = slice(b * 256, (b + 1) * 256)
            a = jnp.dot(pick, hi_scr[:, part], preferred_element_type=F32)
            a_ref[0:OBS, part] = a.astype(BF16)
            square = square + a[:, 0:128] * a[:, 0:128] + a[:, 128:256] * a[:, 128:256]
        mean = jnp.dot(pick, m_scr[...], preferred_element_type=F32)
        lane_o = lax.broadcasted_iota(jnp.int32, (OBS, 128), 1)
        both = jnp.where(
            lane_o == 0,
            jnp.sum(mean, axis=1, keepdims=True),
            jnp.sum(square, axis=1, keepdims=True),
        ).T
        sigma = sigma_ref[...]
        scale = 1.0 / (both[1:2, :] * (1.0 / (M - 1)) + sigma * sigma)
        lines = [local.astype(F32), col.astype(F32)]
        for v in (value_ref[...] - both[0:1, :], sigma, scale):
            lines.extend(halves(v))
        sub = lax.broadcasted_iota(jnp.int32, (16, OBS), 0)
        code = jnp.zeros((16, OBS), F32)
        for i, line in enumerate(lines):
            code = jnp.where(sub == i, line, code)
        a_ref[OBS : OBS + 16, 0:OBS] = code.astype(BF16)
        a_ref[OBS : OBS + 16, OBS:M] = jnp.zeros((16, M - OBS), BF16)


def anomalies(row0, state, pos, side, value, sigma):
    full = lambda shape: pl.BlockSpec(shape, lambda r: (0,) * len(shape))
    tile = pl.BlockSpec((WIDTH, M), lambda r: (r, 0))
    return pl.pallas_call(
        anomaly_kernel,
        grid=(ROWS,),
        in_specs=[pl.BlockSpec(memory_space=pltpu.SMEM), tile, full((2, OBS))]
        + [full((1, OBS))] * 3,
        out_specs=[tile, full((OBS + 16, M))],
        out_shape=[
            jax.ShapeDtypeStruct((CELLS, M), BF16),
            jax.ShapeDtypeStruct((OBS + 16, M), BF16),
        ],
        scratch_shapes=[pltpu.VMEM((CELLS, M), BF16), pltpu.VMEM((CELLS, 128), BF16)],
        compiler_params=pltpu.CompilerParams(
            vmem_limit_bytes=PREP_VMEM, dimension_semantics=("arbitrary",)
        ),
        cost_estimate=cost(1 << 20, 1 << 16),
        name="anomalies",
    )(row0, state, pos, side, value, sigma)


def weights(a_ref, n_ref, w_ref):
    code = a_ref[OBS : OBS + 16, 0:OBS].astype(F32).T
    base = code[:, 2:3] + code[:, 3:4]
    sigma = code[:, 4:5] + code[:, 5:6]
    scale = code[:, 6:7] + code[:, 7:8]
    for i in range(OBS // 32):
        rows = slice(i * 32, (i + 1) * 32)
        w = base[rows] + sigma[rows] * n_ref[rows, :].astype(F32) - a_ref[rows, :].astype(F32)
        w_ref[rows, :] = (w * scale[rows]).astype(BF16)


def covariance(x, a_ref, cov_ref):
    for h in range(2):
        part = slice(h * 256, (h + 1) * 256)
        cov_ref[:, part] = lax.dot_general(
            x, a_ref[part, :], (((1,), (1,)), ((), ())), preferred_element_type=F32
        )


def gain_rows(a_ref, offset, cov_ref, g_ref, unroll):
    code = a_ref[OBS : OBS + 16, 0:OBS].astype(F32)
    col = code[1:2, :] * (1.0 / 16.0)
    n1 = 1.0 / (M - 1)
    row2 = []
    for r in range(ROWS):
        gap = jnp.abs(code[0:1, :] + (ROWS * offset - r).astype(F32))
        row2.append(
            jnp.where(gap > REACH * ROWS, 1e4, jnp.maximum(gap * gap * (1.0 / 256.0), 1e-12))
        )

    @pl.loop(0, WIDTH // CHUNK, unroll=unroll)
    def _(i):
        q = lax.broadcasted_iota(jnp.int32, (CHUNK, 1), 0) + i * CHUNK
        q = q.astype(F32) * (1.0 / 16.0)
        for h in range(2):
            part = slice(h * 256, (h + 1) * 256)
            d = jnp.abs(q - col[:, part])
            d = jnp.minimum(d, 16.0 - d)
            d = d * d
            for r in range(ROWS):
                rows = pl.ds(pl.multiple_of(r * WIDTH + i * CHUNK, CHUNK), CHUNK)
                z2 = d + row2[r][:, part]
                inv = lax.rsqrt(z2)
                z = z2 * inv
                near = (
                    z2 * (z * ((0.625 * n1) + z * ((0.5 * n1) - (0.25 * n1) * z)) - (5.0 / 3.0 * n1))
                    + n1
                )
                u = jnp.maximum(2.0 - z, 0.0)
                u2 = u * u
                far = (u2 * u2) * ((z2 + (2.0 * z - 0.5)) * (inv * (n1 / 12.0)))
                g_ref[rows, part] = (
                    jnp.where(z2 <= 1.0, near, far) * cov_ref[rows, part]
                ).astype(BF16)


def in_vmem():
    return pl.BlockSpec(memory_space=pltpu.VMEM)


def in_smem():
    return pl.BlockSpec(memory_space=pltpu.SMEM)


def contribute_kernel(distances, unroll, sign_ref, x_ref, *refs):
    n = len(distances)
    a_refs = refs[0:n]
    n_refs = refs[n : 2 * n]
    add_refs = refs[2 * n : -4]
    out_ref, cov_scr, g_scr, w_scr = refs[-4:]
    for k in range(n):
        weights(a_refs[k], n_refs[k], w_scr.at[k])

    for k, distance in enumerate(distances):
        covariance(x_ref[...], a_refs[k], cov_scr.at[k])
    for k, distance in enumerate(distances):
        gain_rows(a_refs[k], sign_ref[0] * distance, cov_scr.at[k], g_scr.at[k], unroll)
    for h in range(4):
        part = slice(h * (M // 4), (h + 1) * (M // 4))
        terms = [ref[:, part] for ref in add_refs]
        for k in range(n):
            terms.append(jnp.dot(g_scr[k], w_scr[k, :, part], preferred_element_type=F32))
        out_ref[:, part] = functools.reduce(jnp.add, terms)


def contribute(sign, x, packets, distances, *add, unroll=1):
    n = len(distances)
    return pl.pallas_call(
        functools.partial(contribute_kernel, distances, unroll),
        in_specs=[in_smem()] + [in_vmem()] * (2 * n + 1 + len(add)),
        out_specs=in_vmem(),
        out_shape=jax.ShapeDtypeStruct((CELLS, M), F32),
        scratch_shapes=[
            pltpu.VMEM((n, CELLS, OBS), F32),
            pltpu.VMEM((n, CELLS, OBS), BF16),
            pltpu.VMEM((n, OBS, M), BF16),
        ],
        input_output_aliases={2 + 2 * n: 0} if add else {},
        compiler_params=params(),
        cost_estimate=cost(1 << 20, 1 << 16),
        name="contribute",
    )(sign, x, *[a for a, _ in packets], *[n for _, n in packets], *add)


def gain_kernel(distance, sign_ref, x_ref, a_ref, g_ref, cov_scr):
    covariance(x_ref[...], a_ref, cov_scr)
    gain_rows(a_ref, sign_ref[0] * distance, cov_scr, g_ref, 16)


def gains(sign, x, a, distance):
    return pl.pallas_call(
        functools.partial(gain_kernel, distance),
        in_specs=[in_smem(), in_vmem(), in_vmem()],
        out_specs=in_vmem(),
        out_shape=jax.ShapeDtypeStruct((CELLS, OBS), BF16),
        scratch_shapes=[pltpu.VMEM((CELLS, OBS), F32)],
        compiler_params=params(),
        cost_estimate=cost(1 << 20, 1 << 16),
        name="gains",
    )(sign, x, a)


def edge_kernel(sign_ref, acc_ref, g_ref, a_ref, n_ref, out_ref, cross_ref, inner_ref, w_ref):
    weights(a_ref, n_ref, w_ref)
    for i in range(2):
        here = slice(3 * i * WIDTH, (3 * i + 1) * WIDTH)
        for h in range(4):
            part = slice(h * (M // 4), (h + 1) * (M // 4))
            total = acc_ref[here, part] + jnp.dot(
                g_ref[here, :], w_ref[:, part], preferred_element_type=F32
            )
            out_ref[here, part] = total
            outward = 2 * i - 1 == sign_ref[0]

            @pl.when(jnp.logical_not(outward))
            def _():
                inner_ref[:, part] = total.astype(BF16)

            @pl.when(outward)
            def _():
                cross_ref[:, part] = total.astype(BF16)


def edges(sign, acc, gain, a, noise):
    return pl.pallas_call(
        edge_kernel,
        in_specs=[in_smem()] + [in_vmem()] * 4,
        out_specs=[in_vmem()] * 4,
        out_shape=[
            jax.ShapeDtypeStruct((CELLS, M), F32),
            jax.ShapeDtypeStruct((WIDTH, M), BF16),
            jax.ShapeDtypeStruct((WIDTH, M), BF16),
            jax.ShapeDtypeStruct((OBS, M), BF16),
        ],
        input_output_aliases={1: 0},
        compiler_params=params(),
        cost_estimate=cost(1 << 20, 1 << 16),
        name="edges",
    )(sign, acc, gain, a, noise)


def advance(a, above, below):
    right = pltpu.roll(a, WIDTH - 1, 0)
    left = pltpu.roll(a, 1, 0)
    pull = 0.05 * a * (above - below + (right - left))
    spread = 0.2 * (above + below + right + left - 4.0 * a)
    return a - pull + spread


def middle_kernel(acc_ref, g_ref, w_ref, mid_ref, out_ref, pred_scr, sems):
    rows = lambda r: slice(r * WIDTH, (r + 1) * WIDTH)
    copies = []
    for h in range(4):
        part = slice(h * (M // 4), (h + 1) * (M // 4))
        mids = []
        for i in range(2):
            total = acc_ref[rows(1 + i), part] + jnp.dot(
                g_ref[rows(1 + i), :], w_ref[:, part], preferred_element_type=F32
            )
            mid_ref[rows(i), part] = total
            mids.append(total)
        pred_scr[rows(0), part] = advance(mids[0], mids[1], acc_ref[rows(0), part])
        pred_scr[rows(1), part] = advance(mids[1], acc_ref[rows(3), part], mids[0])
        copies.append(
            pltpu.make_async_copy(
                pred_scr.at[:, part], out_ref.at[WIDTH : 3 * WIDTH, part], sems.at[h]
            )
        )
        copies[-1].start()
    for copy in copies:
        copy.wait()


def middle(acc, gain, w):
    return pl.pallas_call(
        middle_kernel,
        in_specs=[in_vmem()] * 3,
        out_specs=[in_vmem(), pl.BlockSpec(memory_space=pl.ANY)],
        out_shape=[
            jax.ShapeDtypeStruct((2 * WIDTH, M), F32),
            jax.ShapeDtypeStruct((CELLS, M), F32),
        ],
        scratch_shapes=[pltpu.VMEM((2 * WIDTH, M), F32), pltpu.SemaphoreType.DMA((4,))],
        compiler_params=params(),
        cost_estimate=cost(1 << 20, 1 << 16),
        name="middle",
    )(acc, gain, w)


def outer_kernel(sign_ref, acc_ref, mid_ref, cross_ref, inner_ref, _, out_ref, pred_scr, sems):
    rows = lambda r: slice(r * WIDTH, (r + 1) * WIDTH)
    first = sign_ref[0] < 0
    copies = []
    for h in range(4):
        part = slice(h * (M // 4), (h + 1) * (M // 4))
        cross = cross_ref[:, part].astype(F32)
        inner = inner_ref[:, part].astype(F32)
        before = jnp.where(first, cross, inner)
        after = jnp.where(first, inner, cross)
        pred_scr[rows(0), part] = advance(acc_ref[rows(0), part], mid_ref[rows(0), part], before)
        pred_scr[rows(1), part] = advance(acc_ref[rows(3), part], after, mid_ref[rows(1), part])
        for i in range(2):
            copies.append(
                pltpu.make_async_copy(
                    pred_scr.at[rows(i), part], out_ref.at[rows(3 * i), part], sems.at[2 * h + i]
                )
            )
            copies[-1].start()
    for copy in copies:
        copy.wait()


def outer(sign, acc, mid, cross, inner, out):
    return pl.pallas_call(
        outer_kernel,
        in_specs=[in_smem()] + [in_vmem()] * 4 + [pl.BlockSpec(memory_space=pl.ANY)],
        out_specs=pl.BlockSpec(memory_space=pl.ANY),
        out_shape=jax.ShapeDtypeStruct((CELLS, M), F32),
        scratch_shapes=[pltpu.VMEM((2 * WIDTH, M), F32), pltpu.SemaphoreType.DMA((8,))],
        input_output_aliases={5: 0},
        compiler_params=params(),
        cost_estimate=cost(1 << 20, 1 << 16),
        name="outer",
    )(sign, acc, mid, cross, inner, out)


def hold(value, acc):
    held, acc = lax.optimization_barrier((value, acc))
    return held, acc


def on_device(state, obs_value, obs_sigma, obs_noise, obs_pos, obs_side):
    device = lax.axis_index("space")
    slabs = lax.axis_size("space")
    pairs = [(i, i ^ 1) for i in range(slabs)]
    across = [(i, (i + 1 if i % 2 else i - 1) % slabs) for i in range(slabs)]
    inside = lambda block: lax.ppermute(block, "space", pairs)
    beyond = lambda block: lax.ppermute(block, "space", across)
    row0 = (device * ROWS).astype(jnp.int32).reshape(1)
    sign = (2 * (device % 2) - 1).astype(jnp.int32).reshape(1)
    row = lambda v: v.reshape(1, OBS)
    own_n, held = lax.optimization_barrier((obs_noise.astype(BF16), state))
    x, own_a = anomalies(
        row0, held, obs_pos, row(obs_side), row(obs_value), row(obs_sigma)
    )

    one_n, one_a = beyond(own_n), beyond(own_a)
    twin_n, twin_a = inside(own_n), inside(own_a)
    two_a, two_n = beyond(twin_a), beyond(twin_n)
    acc = contribute(sign, x, ((own_a, own_n), (twin_a, twin_n)), (0, -1))
    one_twin_n = inside(one_n)
    one_a, acc, one_twin_n = lax.optimization_barrier((one_a, acc, one_twin_n))
    one_twin_a = inside(one_a)
    one_twin_a, two_a = hold(one_twin_a, two_a)
    three_a, three_n = beyond(one_twin_a), beyond(one_twin_n)
    acc = contribute(sign, x, ((one_a, one_n), (one_twin_a, one_twin_n)), (1, -2), acc, state)
    two_n, acc = hold(two_n, acc)
    two_twin_a, two_twin_n = inside(two_a), inside(two_n)
    two_twin_a, three_a = hold(two_twin_a, three_a)
    four_a, four_n = beyond(two_twin_a), beyond(two_twin_n)
    acc = contribute(sign, x, ((two_a, two_n), (two_twin_a, two_twin_n)), (2, -3), acc)
    three_n, acc = hold(three_n, acc)
    three_twin_a, three_twin_n = inside(three_a), inside(three_n)
    last = ((three_a, three_n), (three_twin_a, three_twin_n))
    acc = contribute(sign, x, last, (3, -4), acc, unroll=16)
    four_a, acc = hold(four_a, acc)
    gain = gains(sign, x, four_a, 4)
    acc, to_cross, to_inner, four_w = edges(sign, acc, gain, four_a, four_n)
    cross, inner = beyond(to_cross), inside(to_inner)
    mid, out = middle(acc, gain, four_w)
    return outer(sign, acc, mid, cross, inner, out)


def solution(mesh):
    placed = (
        P("space", None),
        P("space"),
        P("space"),
        P("space", None),
        P(None, "space"),
        P("space"),
    )
    return jax.shard_map(
        on_device, mesh=mesh, in_specs=placed, out_specs=P("space", None), check_vma=False
    )
```

```python
import functools

import jax
import jax.numpy as jnp
from jax import lax
from jax.experimental import pallas as pl
from jax.experimental.pallas import tpu as pltpu
from jax.sharding import PartitionSpec as P

WIDTH = 256
ROWS = 4
REACH = 4
CELLS = ROWS * WIDTH
OBS = 512
M = 1024
CHUNK = 16
LANES = M // 2
PREP_VMEM = 61 * 1024 * 1024
VMEM = 20 * 1024 * 1024
F32 = jnp.float32
BF16 = jnp.bfloat16


def params():
    return pltpu.CompilerParams(vmem_limit_bytes=VMEM)


def cost(flops, nbytes):
    return pl.CostEstimate(flops=int(flops), bytes_accessed=int(nbytes), transcendentals=0)


def column(row):
    return jnp.broadcast_to(row, (8, row.shape[1])).T[:, 0:1]


def halves(v):
    high = v.astype(BF16).astype(F32)
    return high, v - high


def anomaly_kernel(
    row0_ref, state_ref, pos_ref, side_ref, value_ref, sigma_ref, x_ref, a_ref, hi_scr, m_scr
):
    r = pl.program_id(0)
    s = state_ref[...]
    ms = jnp.mean(s, axis=1, keepdims=True)
    sd = s - ms
    x_ref[...] = sd.astype(BF16)
    dev = 0.5 * (sd + pltpu.roll(sd, WIDTH - 1, 0))
    here = pl.ds(pl.multiple_of(r * WIDTH, WIDTH), WIDTH)
    hi_scr[here, :] = dev.astype(BF16)
    mw = jnp.broadcast_to(ms, (WIDTH, 128))
    pm = 0.5 * (mw + pltpu.roll(mw, WIDTH - 1, 0))
    p0, rest = halves(pm)
    p1, p2 = halves(rest)
    lane = lax.broadcasted_iota(jnp.int32, (WIDTH, 128), 1)
    m_scr[here, :] = jnp.where(
        lane == 0, p0, jnp.where(lane == 1, p1, jnp.where(lane == 2, p2, 0.0))
    ).astype(BF16)

    @pl.when(r == ROWS - 1)
    def _():
        local = pos_ref[0:1, :] - row0_ref[0]
        col = pos_ref[1:2, :]
        left = (col + side_ref[...] - 1) & (WIDTH - 1)
        index = column((local * WIDTH + left).astype(F32)).astype(jnp.int32)
        cells = lax.broadcasted_iota(jnp.int32, (OBS, CELLS), 1)
        pick = jnp.where(cells == index, 1.0, 0.0).astype(BF16)
        square = jnp.zeros((OBS, 128), F32)
        for b in range(4):
            part = slice(b * 256, (b + 1) * 256)
            a = jnp.dot(pick, hi_scr[:, part], preferred_element_type=F32)
            a_ref[0:OBS, part] = a.astype(BF16)
            square = square + a[:, 0:128] * a[:, 0:128] + a[:, 128:256] * a[:, 128:256]
        mean = jnp.dot(pick, m_scr[...], preferred_element_type=F32)
        lane_o = lax.broadcasted_iota(jnp.int32, (OBS, 128), 1)
        both = jnp.where(
            lane_o == 0,
            jnp.sum(mean, axis=1, keepdims=True),
            jnp.sum(square, axis=1, keepdims=True),
        ).T
        sigma = sigma_ref[...]
        scale = 1.0 / (both[1:2, :] * (1.0 / (M - 1)) + sigma * sigma)
        lines = [local.astype(F32), col.astype(F32)]
        for v in (value_ref[...] - both[0:1, :], sigma, scale):
            lines.extend(halves(v))
        sub = lax.broadcasted_iota(jnp.int32, (16, OBS), 0)
        code = jnp.zeros((16, OBS), F32)
        for i, line in enumerate(lines):
            code = jnp.where(sub == i, line, code)
        a_ref[OBS : OBS + 16, 0:OBS] = code.astype(BF16)
        a_ref[OBS : OBS + 16, OBS:M] = jnp.zeros((16, M - OBS), BF16)


def anomalies(row0, state, pos, side, value, sigma):
    full = lambda shape: pl.BlockSpec(shape, lambda r: (0,) * len(shape))
    tile = pl.BlockSpec((WIDTH, M), lambda r: (r, 0))
    return pl.pallas_call(
        anomaly_kernel,
        grid=(ROWS,),
        in_specs=[pl.BlockSpec(memory_space=pltpu.SMEM), tile, full((2, OBS))]
        + [full((1, OBS))] * 3,
        out_specs=[tile, full((OBS + 16, M))],
        out_shape=[
            jax.ShapeDtypeStruct((CELLS, M), BF16),
            jax.ShapeDtypeStruct((OBS + 16, M), BF16),
        ],
        scratch_shapes=[pltpu.VMEM((CELLS, M), BF16), pltpu.VMEM((CELLS, 128), BF16)],
        compiler_params=pltpu.CompilerParams(
            vmem_limit_bytes=PREP_VMEM, dimension_semantics=("arbitrary",)
        ),
        cost_estimate=cost(1 << 20, 1 << 16),
        name="anomalies",
    )(row0, state, pos, side, value, sigma)


def weights(a_ref, n_refs, w_ref):
    code = a_ref[OBS : OBS + 16, 0:OBS].astype(F32).T
    base = code[:, 2:3] + code[:, 3:4]
    sigma = code[:, 4:5] + code[:, 5:6]
    scale = code[:, 6:7] + code[:, 7:8]
    for h, n_ref in n_refs:
        part = slice(h * n_ref.shape[1], (h + 1) * n_ref.shape[1])
        to = part if w_ref.shape[1] == M else slice(0, n_ref.shape[1])
        for i in range(OBS // 32):
            rows = slice(i * 32, (i + 1) * 32)
            w = base[rows] + sigma[rows] * n_ref[rows, :].astype(F32)
            w = w - a_ref[rows, part].astype(F32)
            w_ref[rows, to] = (w * scale[rows]).astype(BF16)


def covariance(x, a_ref, cov_ref):
    for h in range(2):
        part = slice(h * 256, (h + 1) * 256)
        cov_ref[:, part] = lax.dot_general(
            x, a_ref[part, :], (((1,), (1,)), ((), ())), preferred_element_type=F32
        )


def gain_rows(a_ref, offset, cov_ref, g_ref, unroll=1):
    code = a_ref[OBS : OBS + 16, 0:OBS].astype(F32)
    col = code[1:2, :] * (1.0 / 16.0)
    n1 = 1.0 / (M - 1)
    row2 = []
    for r in range(ROWS):
        gap = jnp.abs(code[0:1, :] + (ROWS * offset - r).astype(F32))
        row2.append(
            jnp.where(gap > REACH * ROWS, 1e4, jnp.maximum(gap * gap * (1.0 / 256.0), 1e-12))
        )

    @pl.loop(0, WIDTH // CHUNK, unroll=unroll)
    def _(i):
        q = lax.broadcasted_iota(jnp.int32, (CHUNK, 1), 0) + i * CHUNK
        q = q.astype(F32) * (1.0 / 16.0)
        for h in range(2):
            part = slice(h * 256, (h + 1) * 256)
            d = jnp.abs(q - col[:, part])
            d = jnp.minimum(d, 16.0 - d)
            d = d * d
            for r in range(ROWS):
                rows = pl.ds(pl.multiple_of(r * WIDTH + i * CHUNK, CHUNK), CHUNK)
                z2 = d + row2[r][:, part]
                inv = lax.rsqrt(z2)
                z = z2 * inv
                near = (
                    z2 * (z * ((0.625 * n1) + z * ((0.5 * n1) - (0.25 * n1) * z)) - (5.0 / 3.0 * n1))
                    + n1
                )
                u = jnp.maximum(2.0 - z, 0.0)
                u2 = u * u
                far = (u2 * u2) * ((z2 + (2.0 * z - 0.5)) * (inv * (n1 / 12.0)))
                g_ref[rows, part] = (
                    jnp.where(z2 <= 1.0, near, far) * cov_ref[rows, part]
                ).astype(BF16)


def in_vmem():
    return pl.BlockSpec(memory_space=pltpu.VMEM)


def in_smem():
    return pl.BlockSpec(memory_space=pltpu.SMEM)


def contribute_kernel(distances, counts, unroll, sign_ref, x_ref, *refs):
    n = len(distances)
    a_refs = refs[0:n]
    refs = refs[n:]
    out_ref, cov_scr, g_scr, w_scr = refs[-4:]
    for k in range(n):
        weights(a_refs[k], list(enumerate(refs[0 : counts[k]])), w_scr.at[k])
        refs = refs[counts[k] :]
    add_refs = refs[:-4]
    for k, distance in enumerate(distances):
        covariance(x_ref[...], a_refs[k], cov_scr.at[k])
    for k, distance in enumerate(distances):
        gain_rows(a_refs[k], sign_ref[0] * distance, cov_scr.at[k], g_scr.at[k], unroll)
    for h in range(4):
        part = slice(h * (M // 4), (h + 1) * (M // 4))
        terms = [ref[:, part] for ref in add_refs]
        for k in range(n):
            terms.append(jnp.dot(g_scr[k], w_scr[k, :, part], preferred_element_type=F32))
        out_ref[:, part] = functools.reduce(jnp.add, terms)


def contribute(sign, x, packets, distances, *add, unroll=1):
    n = len(distances)
    blocks = [a for a, _ in packets]
    for _, parts in packets:
        blocks.extend(parts)
    return pl.pallas_call(
        functools.partial(
            contribute_kernel, distances, [len(parts) for _, parts in packets], unroll
        ),
        in_specs=[in_smem()] + [in_vmem()] * (1 + len(blocks) + len(add)),
        out_specs=in_vmem(),
        out_shape=jax.ShapeDtypeStruct((CELLS, M), F32),
        scratch_shapes=[
            pltpu.VMEM((n, CELLS, OBS), F32),
            pltpu.VMEM((n, CELLS, OBS), BF16),
            pltpu.VMEM((n, OBS, M), BF16),
        ],
        input_output_aliases={2 + len(blocks): 0} if add else {},
        compiler_params=params(),
        cost_estimate=cost(1 << 20, 1 << 16),
        name="contribute",
    )(sign, x, *blocks, *add)


def gain_kernel(distance, sign_ref, x_ref, a_ref, g_ref, cov_scr):
    covariance(x_ref[...], a_ref, cov_scr)
    gain_rows(a_ref, sign_ref[0] * distance, cov_scr, g_ref, 16)


def gains(sign, x, a, distance):
    return pl.pallas_call(
        functools.partial(gain_kernel, distance),
        in_specs=[in_smem(), in_vmem(), in_vmem()],
        out_specs=in_vmem(),
        out_shape=jax.ShapeDtypeStruct((CELLS, OBS), BF16),
        scratch_shapes=[pltpu.VMEM((CELLS, OBS), F32)],
        compiler_params=params(),
        cost_estimate=cost(1 << 20, 1 << 16),
        name="gains",
    )(sign, x, a)


def edge_kernel(half, sign_ref, acc_ref, g_ref, a_ref, n_ref, out_ref, cross_ref, inner_ref, w_ref):
    weights(a_ref, [(half, n_ref)], w_ref)
    for i in range(2):
        here = slice(3 * i * WIDTH, (3 * i + 1) * WIDTH)
        outward = 2 * i - 1 == sign_ref[0]
        for h in range(2):
            part = slice(h * 256, (h + 1) * 256)
            total = acc_ref[here, half * LANES + h * 256 : half * LANES + (h + 1) * 256]
            total = total + jnp.dot(g_ref[here, :], w_ref[:, part], preferred_element_type=F32)
            out_ref[i * WIDTH : (i + 1) * WIDTH, part] = total

            @pl.when(jnp.logical_not(outward))
            def _():
                inner_ref[:, part] = total.astype(BF16)

            @pl.when(outward)
            def _():
                cross_ref[:, part] = total.astype(BF16)


def edges(sign, acc, gain, a, noise, half):
    return pl.pallas_call(
        functools.partial(edge_kernel, half),
        in_specs=[in_smem()] + [in_vmem()] * 4,
        out_specs=[in_vmem()] * 4,
        out_shape=[
            jax.ShapeDtypeStruct((2 * WIDTH, LANES), F32),
            jax.ShapeDtypeStruct((WIDTH, LANES), BF16),
            jax.ShapeDtypeStruct((WIDTH, LANES), BF16),
            jax.ShapeDtypeStruct((OBS, LANES), BF16),
        ],
        compiler_params=params(),
        cost_estimate=cost(1 << 20, 1 << 16),
        name="edges",
    )(sign, acc, gain, a, noise)


def advance(a, above, below):
    right = pltpu.roll(a, WIDTH - 1, 0)
    left = pltpu.roll(a, 1, 0)
    pull = 0.05 * a * (above - below + (right - left))
    spread = 0.2 * (above + below + right + left - 4.0 * a)
    return a - pull + spread


def middle_kernel(half, acc_ref, g_ref, w_ref, edge_ref, *refs):
    mid_ref, out_ref, pred_scr, sems = refs[-4:]
    rows = lambda r: slice(r * WIDTH, (r + 1) * WIDTH)
    copies = []
    for h in range(2):
        part = slice(h * 256, (h + 1) * 256)
        far = slice(half * LANES + h * 256, half * LANES + (h + 1) * 256)
        mids = []
        for i in range(2):
            total = acc_ref[rows(1 + i), far] + jnp.dot(
                g_ref[rows(1 + i), :], w_ref[:, part], preferred_element_type=F32
            )
            mid_ref[rows(i), part] = total
            mids.append(total)
        pred_scr[rows(0), part] = advance(mids[0], mids[1], edge_ref[rows(0), part])
        pred_scr[rows(1), part] = advance(mids[1], edge_ref[rows(1), part], mids[0])
        copies.append(
            pltpu.make_async_copy(
                pred_scr.at[:, part], out_ref.at[WIDTH : 3 * WIDTH, far], sems.at[h]
            )
        )
        copies[-1].start()
    for copy in copies:
        copy.wait()


def middle(acc, gain, w, edge, half, *out):
    return pl.pallas_call(
        functools.partial(middle_kernel, half),
        in_specs=[in_vmem()] * 4 + [pl.BlockSpec(memory_space=pl.ANY)] * len(out),
        out_specs=[in_vmem(), pl.BlockSpec(memory_space=pl.ANY)],
        out_shape=[
            jax.ShapeDtypeStruct((2 * WIDTH, LANES), F32),
            jax.ShapeDtypeStruct((CELLS, M), F32),
        ],
        scratch_shapes=[pltpu.VMEM((2 * WIDTH, LANES), F32), pltpu.SemaphoreType.DMA((2,))],
        input_output_aliases={4: 1} if out else {},
        compiler_params=params(),
        cost_estimate=cost(1 << 20, 1 << 16),
        name="middle",
    )(acc, gain, w, edge, *out)


def outer_kernel(
    half, sign_ref, edge_ref, mid_ref, cross_ref, inner_ref, _, out_ref, pred_scr, sems
):
    rows = lambda r: slice(r * WIDTH, (r + 1) * WIDTH)
    first = sign_ref[0] < 0
    copies = []
    for h in range(2):
        part = slice(h * 256, (h + 1) * 256)
        far = slice(half * LANES + h * 256, half * LANES + (h + 1) * 256)
        cross = cross_ref[:, part].astype(F32)
        inner = inner_ref[:, part].astype(F32)
        before = jnp.where(first, cross, inner)
        after = jnp.where(first, inner, cross)
        pred_scr[rows(0), part] = advance(edge_ref[rows(0), part], mid_ref[rows(0), part], before)
        pred_scr[rows(1), part] = advance(edge_ref[rows(1), part], after, mid_ref[rows(1), part])
        for i in range(2):
            copies.append(
                pltpu.make_async_copy(
                    pred_scr.at[rows(i), part], out_ref.at[rows(3 * i), far], sems.at[2 * h + i]
                )
            )
            copies[-1].start()
    for copy in copies:
        copy.wait()


def outer(sign, edge, mid, cross, inner, half, out):
    return pl.pallas_call(
        functools.partial(outer_kernel, half),
        in_specs=[in_smem()] + [in_vmem()] * 4 + [pl.BlockSpec(memory_space=pl.ANY)],
        out_specs=pl.BlockSpec(memory_space=pl.ANY),
        out_shape=jax.ShapeDtypeStruct((CELLS, M), F32),
        scratch_shapes=[pltpu.VMEM((2 * WIDTH, LANES), F32), pltpu.SemaphoreType.DMA((4,))],
        input_output_aliases={5: 0},
        compiler_params=params(),
        cost_estimate=cost(1 << 20, 1 << 16),
        name="outer",
    )(sign, edge, mid, cross, inner, out)


def hold(value, acc):
    held, acc = lax.optimization_barrier((value, acc))
    return held, acc


def on_device(state, obs_value, obs_sigma, obs_noise, obs_pos, obs_side):
    device = lax.axis_index("space")
    slabs = lax.axis_size("space")
    pairs = [(i, i ^ 1) for i in range(slabs)]
    across = [(i, (i + 1 if i % 2 else i - 1) % slabs) for i in range(slabs)]
    inside = lambda block: lax.ppermute(block, "space", pairs)
    beyond = lambda block: lax.ppermute(block, "space", across)
    row0 = (device * ROWS).astype(jnp.int32).reshape(1)
    sign = (2 * (device % 2) - 1).astype(jnp.int32).reshape(1)
    row = lambda v: v.reshape(1, OBS)
    own_n, held = lax.optimization_barrier((obs_noise.astype(BF16), state))
    x, own_a = anomalies(
        row0, held, obs_pos, row(obs_side), row(obs_value), row(obs_sigma)
    )

    one_n, one_a = beyond(own_n), beyond(own_a)
    twin_n, twin_a = inside(own_n), inside(own_a)
    two_a, two_n = beyond(twin_a), beyond(twin_n)
    acc = contribute(sign, x, ((own_a, (own_n,)), (twin_a, (twin_n,))), (0, -1))
    one_twin_n = inside(one_n)
    one_a, acc, one_twin_n = lax.optimization_barrier((one_a, acc, one_twin_n))
    one_twin_a = inside(one_a)
    one_twin_a, two_a = hold(one_twin_a, two_a)
    three_a, three_n = beyond(one_twin_a), beyond(one_twin_n)
    acc = contribute(sign, x, ((one_a, (one_n,)), (one_twin_a, (one_twin_n,))), (1, -2), acc, state)
    two_n, acc = hold(two_n, acc)
    two_twin_a = inside(two_a)
    two_twin_n = [inside(two_n[:, h * LANES : (h + 1) * LANES]) for h in range(2)]
    two_twin_a, three_a = hold(two_twin_a, three_a)
    four_a, four_n = beyond(two_twin_a), [beyond(n) for n in two_twin_n]
    acc = contribute(sign, x, ((two_a, (two_n,)), (two_twin_a, two_twin_n)), (2, -3), acc)
    three_n, acc = hold(three_n, acc)
    three_twin_a, three_twin_n = inside(three_a), inside(three_n)
    last = ((three_a, (three_n,)), (three_twin_a, (three_twin_n,)))
    acc = contribute(sign, x, last, (3, -4), acc, unroll=16)
    four_a, acc = hold(four_a, acc)
    gain = gains(sign, x, four_a, 4)
    done = []
    out = ()
    for half in range(2):
        edge, to_cross, to_inner, w = edges(sign, acc, gain, four_a, four_n[half], half)
        cross, inner = beyond(to_cross), inside(to_inner)
        mid, *out = middle(acc, gain, w, edge, half, *out)
        done.append((edge, mid, cross, inner))
    out = out[0]
    for half in range(2):
        out = outer(sign, *done[half], half, out)
    return out


def solution(mesh):
    placed = (
        P("space", None),
        P("space"),
        P("space"),
        P("space", None),
        P(None, "space"),
        P("space"),
    )
    return jax.shard_map(
        on_device, mesh=mesh, in_specs=placed, out_specs=P("space", None), check_vma=False
    )
```
